512 devices in a mesh: gx: 32 (over z_hi, y), gy: 4 (over z_lo, core), pa: 4 (over x).
Axes of the slice: x: 4, y: 8, z: 8 (z_hi: 4, z_lo: 2; z = z_hi * 2 + z_lo), core: 2. Of those that a mesh axis runs over, the one named last changes fastest.
Arguments:
- latents: bfloat16 [512, 128, 768], P(('gx', 'pa'), 'gy'), may hold values from -6 to 6
- noise: bfloat16 [2, 512, 128, 768], P(None, ('gx', 'pa'), 'gy'), may hold values from -6 to 6
- proc_gain: float32 [768], replicated, may hold values from 0.1 to 1.9
- w_qkv: bfloat16 [768, 2304], P(('gx', 'pa')), may hold values from -0.21875 to 0.21875
- w_out: bfloat16 [768, 768], P(('gx', 'pa')), may hold values from -0.21875 to 0.21875
- w_query: bfloat16 [128, 768], P(('gx', 'pa')), may hold values from -0.5 to 0.5
- w_head: bfloat16 [768, 3], P(('gx', 'pa')), may hold values from -0.21875 to 0.21875
- probe_cell: int32 [524288], P(('gx', 'gy', 'pa')), may hold values from 0 to 127
- probe_offset: float32 [2, 524288], P(None, ('gx', 'gy', 'pa')), may hold values from 0 to 1
- probe_count: int32 [512], P(('gx', 'gy', 'pa')), may hold values from 128 to 1024, as said below
Outputs:
- latent_out: bfloat16 [512, 128, 768], P(('gx', 'pa'), 'gy')
- probe_values: float32 [3, 524288], P(None, ('gx', 'gy', 'pa'))
The draws below stay inside these ranges and needn't reach their ends.
Inputs may be any that keep to these rules, and one draw needn't show every extreme that they name: `probe_cell`: a cell of the device's own 4 x 32 block, numbered row by row. `probe_count`: slots below the count hold probes, the others are empty; in every draw one device has all 1024 slots live.
All inputs are finite; a program needn't handle non-finite values.
Results may differ from the reference program's by a relative error of at most 0.02.
Values may be sent and summed in bfloat16 or wider, within the bound.
No kernel may reach another device: no remote copies, remote signals or barrier semaphores. Data moves between devices by JAX's collectives and lax.ppermute only.
A program may use at most 64 MiB of HBM per device.

```python
import math
import jax
import jax.numpy as jnp
from jax import lax

D = 768
HEADS = 12
FQ = 128
CH = 3
RAD = 3
STEPS = 2
ROWS = 4
COLS = 32
PCAP = 1024
LX = 512
LY = 128
NPROBE = 524288
N_GY = 4
N_PA = 4


def draw_probe_count(key, part):
    device_total = NPROBE // PCAP
    first, second, third = jax.random.split(jax.random.fold_in(key, 11), 3)
    counts = jax.random.randint(first, (device_total,), PCAP // 8, PCAP + 1)
    fullest = jax.random.randint(second, (), 0, device_total)
    sparse = (fullest + 1 + jax.random.randint(third, (), 0, device_total - 1)) % device_total
    places = jnp.arange(device_total, dtype=jnp.int32)
    counts = jnp.where(places == sparse, PCAP // 8, counts)
    counts = jnp.where(places == fullest, PCAP, counts)
    return counts.astype(jnp.int32)


def touch_ends(array, own_key, low, top_value):
    longest = array.shape.index(max(array.shape))
    spots = []
    for shift in (0, 1):
        where = [jax.random.randint(jax.random.fold_in(own_key, axis), (), 0, length) for axis, length in enumerate(array.shape)]
        where[longest] = (where[longest] + shift) % array.shape[longest]
        spots.append(tuple(where))
    return array.at[spots[0]].set(low).at[spots[1]].set(top_value)


def level_of(key, extent, cuts, smallest, top_value):
    loudness, own = 1.0, jax.random.fold_in(key, 6)
    for dim, parts in cuts:
        steps = jnp.exp(jax.random.uniform(jax.random.fold_in(own, dim), (parts,), jnp.float32, smallest / len(cuts), top_value / len(cuts)))
        loudness = loudness * jnp.repeat(steps, extent[dim] // parts).reshape([-1 if axis == dim else 1 for axis in range(len(extent))])
    return loudness


def bell_draw(key, dims, deviation, bound, pieces=(), held_as=jnp.bfloat16):
    gain = level_of(key, dims, pieces, -0.22, 0.18) if pieces else 1.0
    drawn = jax.random.normal(key, dims, jnp.float32) * deviation * gain
    return jnp.minimum(jnp.maximum(drawn, -bound), bound).astype(held_as)


def setup_inputs(seed: int = 0) -> dict:
    streams_of = jax.random.split(jax.random.key(seed), 11)
    return {
        "latents": bell_draw(streams_of[0], (LX, LY, D), 1.0, 6.0, ((0, 128), (1, 4))),
        "noise": bell_draw(streams_of[1], (STEPS, LX, LY, D), 1.0, 6.0, ((1, 128), (2, 4))),
        "proc_gain": jnp.clip(1.0 + 0.18 * jax.random.normal(streams_of[2], (D,), jnp.float32), 0.1, 1.9),
        "w_qkv": bell_draw(streams_of[3], (D, 3 * D), D ** -0.5, 0.21875, ((0, 128),)),
        "w_out": bell_draw(streams_of[4], (D, D), D ** -0.5, 0.21875, ((0, 128),)),
        "w_query": bell_draw(streams_of[5], (FQ, D), FQ ** -0.5, 0.5, ((0, 128),)),
        "w_head": bell_draw(streams_of[6], (D, CH), D ** -0.5, 0.21875, ((0, 128),)),
        "probe_cell": touch_ends(jax.random.randint(streams_of[7], (NPROBE,), 0, ROWS * COLS), jax.random.fold_in(streams_of[7], 1), 0, (ROWS * COLS) - 1).astype(jnp.int32),
        "probe_offset": jnp.clip(1.0 * jax.random.uniform(streams_of[8], (2, NPROBE), jnp.float32) ** level_of(streams_of[8], (2, NPROBE), ((1, 512),), -0.2, 0.2), 0.0, 1.0),
        "probe_count": draw_probe_count(jax.random.fold_in(streams_of[10], 71), 0),
    }


EPS = 1e-06
NOISE_COEF = 0.3

def normalize(tokens, gain_vec):
    values = tokens.astype(jnp.float32)
    factor = lax.rsqrt(lax.optimization_barrier(jnp.mean(values * values, axis=-1, keepdims=True)) + EPS)
    return (values * factor * gain_vec.astype(jnp.float32)).astype(jnp.bfloat16)

def neighbour_attention(queries, key_values, row_count, col_count):
    model_width = queries.shape[-1]
    head_size = model_width // HEADS
    window_span = 2 * RAD + 1
    query_four = queries.astype(jnp.float32).reshape(row_count, col_count, HEADS, head_size)
    score_list = []
    for row_step in range(window_span):
        for col_step in range(window_span):
            key_rows = key_values[row_step:row_step + row_count, col_step:col_step + col_count, :model_width]
            key_four = key_rows.astype(jnp.float32).reshape(row_count, col_count, HEADS, head_size)
            score_list.append(jnp.einsum('rchd,rchd->rch', query_four, key_four) / math.sqrt(head_size))
    scores = jnp.stack(score_list)
    weights = jax.nn.softmax(scores, axis=0).astype(jnp.bfloat16)
    summed = jnp.zeros((row_count, col_count, HEADS, head_size), jnp.float32)
    for row_step in range(window_span):
        for col_step in range(window_span):
            value_rows = key_values[row_step:row_step + row_count, col_step:col_step + col_count, model_width:]
            value_four = value_rows.astype(jnp.float32).reshape(row_count, col_count, HEADS, head_size)
            weight_now = weights[row_step * window_span + col_step].astype(jnp.float32)
            summed = summed + weight_now[..., None] * value_four
    return summed.reshape(row_count, col_count, model_width).astype(jnp.bfloat16)

def wrap_extend(grid, depth):
    grid = jnp.concatenate([grid[-depth:], grid, grid[:depth]], axis=0)
    return jnp.concatenate([grid[:, -depth:], grid, grid[:, :depth]], axis=1)

def decode_block(context, offsets, w_query, w_head):
    block_size = context.shape[0]
    model_width = context.shape[-1]
    head_size = model_width // HEADS
    freq = jnp.arange(1, FQ // 4 + 1, dtype=jnp.float32)
    angle_x = 2.0 * math.pi * offsets[0][:, None] * freq[None, :]
    angle_y = 2.0 * math.pi * offsets[1][:, None] * freq[None, :]
    features = jnp.concatenate([jnp.sin(angle_x), jnp.cos(angle_x), jnp.sin(angle_y), jnp.cos(angle_y)], axis=1).astype(jnp.bfloat16)
    probe_query = jnp.dot(features, w_query, preferred_element_type=jnp.float32).astype(jnp.bfloat16)
    query_three = probe_query.astype(jnp.float32).reshape(block_size, HEADS, head_size)
    context_four = context.astype(jnp.float32).reshape(block_size, 9, HEADS, head_size)
    scores = jnp.einsum('phd,pmhd->pmh', query_three, context_four) / math.sqrt(head_size)
    weights = jax.nn.softmax(scores, axis=1).astype(jnp.bfloat16)
    mixed = jnp.einsum('pmh,pmhd->phd', weights.astype(jnp.float32), context_four)
    mixed = mixed.reshape(block_size, model_width).astype(jnp.bfloat16)
    return jnp.dot(mixed, w_head, preferred_element_type=jnp.float32)

def reference(latents, noise, proc_gain, w_qkv, w_out, w_query, w_head, probe_cell, probe_offset, probe_count):
    grid_rows, grid_cols, model_width = latents.shape
    latent = latents
    for step in range(STEPS):
        normed = normalize(latent, proc_gain)
        triple = lax.map(lambda row_tokens: jnp.dot(row_tokens, w_qkv, preferred_element_type=jnp.float32).astype(jnp.bfloat16), normed)
        queries = triple[..., :model_width]
        key_values = wrap_extend(triple[..., model_width:], RAD)

        def one_row(index):
            rows_in = lax.dynamic_slice_in_dim(key_values, index, 2 * RAD + 1, 0)
            row_query = lax.dynamic_slice_in_dim(queries, index, 1, 0)
            attended = neighbour_attention(row_query, rows_in, 1, grid_cols)
            return jnp.dot(attended[0], w_out, preferred_element_type=jnp.float32)
        updates = lax.map(one_row, jnp.arange(grid_rows, dtype=jnp.int32))
        latent = (latent.astype(jnp.float32) + updates / STEPS + NOISE_COEF * noise[step].astype(jnp.float32)).astype(jnp.bfloat16)
    final_ext = wrap_extend(latent, 1)
    flat_ext = final_ext.reshape(-1, model_width)
    slots = jnp.arange(NPROBE, dtype=jnp.int32)
    device = slots // PCAP
    pa_index = device % N_PA
    gy_index = device // N_PA % N_GY
    gx_index = device // (N_PA * N_GY)
    grid_row = (gx_index * N_PA + pa_index) * ROWS + probe_cell // COLS
    grid_col = gy_index * COLS + probe_cell % COLS
    index_list = []
    for row_step in range(3):
        for col_step in range(3):
            index_list.append((grid_row + row_step) * (grid_cols + 2) + grid_col + col_step)
    cell_index = jnp.stack(index_list, axis=1).astype(jnp.int32)
    block_size = min(256, PCAP)
    block_count = NPROBE // block_size

    def one_block(start):
        rows_index = lax.dynamic_slice_in_dim(cell_index, start, block_size, 0)
        context = jnp.take(flat_ext, rows_index, axis=0)
        offsets = lax.dynamic_slice_in_dim(probe_offset, start, block_size, 1)
        return decode_block(context, offsets, w_query, w_head)
    starts = jnp.arange(block_count, dtype=jnp.int32) * block_size
    values = lax.map(one_block, starts).reshape(NPROBE, CH)
    live = slots % PCAP < probe_count[device]
    probe_values = jnp.where(live[None, :], values.T, jnp.zeros((), jnp.float32))
    return (latent, probe_values)
```

```python
import math

import jax
import jax.numpy as jnp
import numpy as np
from jax import lax
from jax.experimental import pallas as pl
from jax.experimental.pallas import tpu as pltpu
from jax.sharding import PartitionSpec as P

HEADS = 12
FQ = 128
CH = 3
RAD = 3
STEPS = 2
EPS = 1e-06
NOISE_COEF = 0.3

WIDTH = 768
ROWS = 4
COLS = 32
HALO0 = 2 * RAD + 1
HALO1 = RAD + 1
KEY_ROWS = ROWS + 2 * HALO0
KEY_COLS = COLS + 2 * HALO0
PITCH0 = 48
MID_ROWS = ROWS + 2 * HALO1
PITCH1 = COLS + 2 * HALO1
END_ROWS = ROWS + 2
N_KEY0 = KEY_ROWS * PITCH0
N_MID = MID_ROWS * PITCH1
N_END = END_ROWS * PITCH1
PAIR = 2 * PITCH1
KEYS = 384
HALF = 1664
NEG = -1e30
SCALE = math.log2(math.e) / 8.0

BF = jnp.bfloat16
F32 = jnp.float32


def permutation_tables():
    target = np.arange(WIDTH)
    lane, rest = target // 192, target % 192
    source = (rest // 6) * 24 + lane * 6 + rest % 6
    perm = np.zeros((WIDTH, WIDTH), np.float32)
    perm[source, target] = 1.0
    pick = np.zeros((WIDTH, WIDTH), np.float32)
    out = np.arange(WIDTH)
    pick[out, (out % 128) * 6 + out // 128] = 1.0
    return perm, pick


def rms(values, gain):
    factor = lax.rsqrt(jnp.mean(values * values, axis=-1, keepdims=True) + EPS)
    return (values * factor * gain).astype(BF)


def prep_kernel(x0_ref, xq_ref, gain_ref, perm_ref, nk_ref, nq_ref):
    gain = gain_ref[...]
    for src, dst, chunk in ((x0_ref, nk_ref, 288), (xq_ref, nq_ref, 240)):
        for start in range(0, src.shape[0], chunk):
            normed = rms(src[start : start + chunk].astype(F32), gain)
            dst[start : start + chunk] = jnp.dot(
                normed, perm_ref[...], preferred_element_type=F32
            ).astype(BF)


def stair(index, step, count):
    total = jnp.zeros(index.shape, jnp.int32)
    for i in range(1, count):
        total = total + (index >= step * i).astype(jnp.int32)
    return total


def window_mask(pitch, rows_of_keys):
    row = lax.broadcasted_iota(jnp.int32, (PAIR, KEYS), 0)
    lane = lax.broadcasted_iota(jnp.int32, (PAIR, KEYS), 1)
    q_row = stair(row, PITCH1, 2)
    q_col = row - PITCH1 * q_row
    k_row = stair(lane, pitch, rows_of_keys)
    k_col = lane - pitch * k_row
    return q_row, q_col, k_row, k_col


def attend(queries, keys, values, mask):
    lane_head = stair(lax.broadcasted_iota(jnp.int32, (PAIR, 256), 1), 64, 4)
    zero = jnp.zeros((), BF)
    stacked = jnp.concatenate(
        [jnp.where(lane_head == h, queries, zero) for h in range(4)], axis=0
    )
    scores = lax.dot_general(
        stacked, keys, (((1,), (1,)), ((), ())), preferred_element_type=F32
    )
    parts = []
    for h in range(4):
        part = scores[h * PAIR : (h + 1) * PAIR] + mask
        top = jnp.max(part, axis=1, keepdims=True)
        weight = jnp.exp2((part - top) * SCALE)
        total = jnp.sum(weight, axis=1, keepdims=True)
        parts.append((weight.astype(BF), total))
    mixed = jnp.dot(
        jnp.concatenate([p[0] for p in parts], axis=0), values, preferred_element_type=F32
    )
    result = jnp.zeros((PAIR, 256), F32)
    for h in range(4):
        result = jnp.where(
            lane_head == h, mixed[h * PAIR : (h + 1) * PAIR] / parts[h][1], result
        )
    return result.astype(BF)


def main_kernel(
    place_ref,
    nk_ref,
    nq_ref,
    xq_ref,
    n0_ref,
    n1_ref,
    gain_ref,
    feat_ref,
    cell_ref,
    perm_ref,
    pick_ref,
    own_a,
    low_a,
    high_a,
    top_a,
    bot_a,
    own_b,
    low_b,
    high_b,
    top_b,
    bot_b,
    latent_ref,
    probe_ref,
    weights,
    keys,
    values,
    q_low,
    q_wide,
    att,
    att_perm,
    lat_mid,
    mid_perm,
    lat_end,
    end_heads,
    end_turned,
    probe_query,
    mixed_ref,
    sems,
):
    lane = place_ref[0]
    core = place_ref[1]
    live = place_ref[2]
    copies = []
    for slot, group in ((core, (own_a, low_a, high_a, top_a, bot_a)), (1 - core, (own_b, low_b, high_b, top_b, bot_b))):
        spots = (
            lax.rem(lane, 4) * 192,
            lax.rem(lane + 3, 4) * 192,
            lax.rem(lane + 1, 4) * 192,
            lax.rem(lane + 2, 4) * 192,
            lax.rem(lane + 2, 4) * 192 + 96,
        )
        for ref, start in zip(group, spots):
            copy = pltpu.make_async_copy(
                ref,
                weights.at[slot, pl.ds(pl.multiple_of(start, 96), ref.shape[0])],
                sems.at[len(copies)],
            )
            copy.start()
            copies.append(copy)
    for copy in copies:
        copy.wait()

    def project(source, which, column, target, rows, low=True):
        def tile(t, carry):
            offset = pl.multiple_of(t * 256, 256)
            product = jnp.dot(
                source[...],
                weights[which, :, pl.ds(column + offset, 256)],
                preferred_element_type=F32,
            ).astype(BF)
            target[0:rows, pl.ds(offset, 256)] = product.astype(target.dtype)
            return carry

        lax.fori_loop(0, 3, tile, 0)

    def permute_into(source, target, rows):
        target[0:rows] = jnp.dot(
            source[0:rows], perm_ref[...], preferred_element_type=F32
        ).astype(BF)

    project(nk_ref, 0, 0, keys, N_KEY0)
    project(nk_ref, 0, 768, values, N_KEY0)
    project(nq_ref, 1, 0, q_low, N_MID)

    q_row, q_col, k_row, k_col = window_mask(PITCH0, 8)
    inside = (
        (k_row >= q_row)
        & (k_row <= q_row + 2 * RAD)
        & (k_col >= q_col)
        & (k_col <= q_col + 2 * RAD)
    )
    mask = jnp.where(inside, 0.0, NEG).astype(F32)

    def attend0(j, carry):
        q_at = pl.multiple_of(j * PAIR, PAIR)
        k_at = pl.multiple_of(j * 2 * PITCH0, 2 * PITCH0)
        for g in range(3):
            cols = slice(256 * g, 256 * g + 256)
            att[pl.ds(q_at, PAIR), cols] = attend(
                q_low[pl.ds(q_at, PAIR), cols],
                keys[pl.ds(k_at, KEYS), cols],
                values[pl.ds(k_at, KEYS), cols],
                mask,
            )
        return carry

    lax.fori_loop(0, MID_ROWS // 2, attend0, 0)
    permute_into(att, att_perm, N_MID)

    for t in range(3):
        cols = slice(256 * t, 256 * t + 256)
        update = jnp.dot(
            att_perm[...],
            weights[1, :, 768 + 256 * t : 1024 + 256 * t],
            preferred_element_type=F32,
        )
        fresh = (
            xq_ref[:, cols].astype(F32)
            + update / STEPS
            + NOISE_COEF * n0_ref[:, cols].astype(F32)
        )
        lat_mid[:, cols] = fresh.astype(BF).astype(F32)

    mid_perm[...] = jnp.dot(
        rms(lat_mid[...], gain_ref[...]), perm_ref[...], preferred_element_type=F32
    ).astype(BF)
    project(mid_perm, 0, 0, keys, N_MID)
    project(mid_perm, 0, 768, values, N_MID)
    project(mid_perm.at[112:368], 1, 0, q_wide, 256)

    q_row, q_col, k_row, k_col = window_mask(PITCH1, 10)
    inside = (
        (k_row >= q_row)
        & (k_row <= q_row + 2 * RAD)
        & (k_col >= q_col - RAD)
        & (k_col <= q_col + RAD)
    )
    mask = jnp.where(inside, 0.0, NEG).astype(F32)

    def attend1(j, carry):
        at = pl.multiple_of(j * PAIR, PAIR)
        for g in range(3):
            cols = slice(256 * g, 256 * g + 256)
            att[pl.ds(at, PAIR), cols] = attend(
                q_wide[pl.ds(pl.multiple_of(at + 8, 8), PAIR), cols].astype(BF),
                keys[pl.ds(at, KEYS), cols],
                values[pl.ds(at, KEYS), cols],
                mask,
            )
        return carry

    lax.fori_loop(0, END_ROWS // 2, attend1, 0)
    permute_into(att, att_perm, N_END)

    lat_end[N_END:] = jnp.zeros((256 - N_END, WIDTH), F32)
    for t in range(3):
        cols = slice(256 * t, 256 * t + 256)
        update = jnp.dot(
            att_perm[0:N_END],
            weights[1, :, 768 + 256 * t : 1024 + 256 * t],
            preferred_element_type=F32,
        )
        fresh = (
            lat_mid[3 * PITCH1 : 3 * PITCH1 + N_END, cols]
            + update / STEPS
            + NOISE_COEF * n1_ref[:, cols].astype(F32)
        )
        lat_end[0:N_END, cols] = fresh.astype(BF).astype(F32)
    for r in range(ROWS):
        start = PITCH1 * (r + 1) + HALO1
        latent_ref[COLS * r : COLS * r + COLS] = lat_end[start : start + COLS].astype(BF)

    lane_head = stair(lax.broadcasted_iota(jnp.int32, (256, 256), 1), 64, 4)
    for g in range(3):
        quad = lat_end[:, 256 * g : 256 * g + 256]
        low = quad.astype(BF)
        for h in range(4):
            end_heads[4 * g + h] = jnp.where(lane_head == h, low, jnp.zeros((), BF))
        end_turned[256 * g : 256 * g + 256] = quad.T.astype(BF)

    query_rows = jnp.dot(
        pick_ref[...], weights[1, :, 1536:1664], preferred_element_type=F32
    )
    for i in range(6):
        block = query_rows[128 * i : 128 * i + 128].T.astype(BF)
        probe_query[128 * i : 128 * i + 128] = jnp.dot(
            block, feat_ref[...], preferred_element_type=F32
        ).astype(BF)
    head_rows = jnp.dot(perm_ref[...], weights[0, :, 1536:1664], preferred_element_type=F32)
    head_turned = head_rows.T.astype(BF)

    spot = lax.broadcasted_iota(jnp.int32, (256, 256), 0)
    spot_row = stair(spot, PITCH1, 7)
    spot_col = spot - PITCH1 * spot_row

    def decode(b, carry):
        at = pl.multiple_of(b * 256, 256)
        cell = cell_ref[:, pl.ds(at, 256)]
        cell_row = lax.shift_right_logical(cell, 5)
        cell_col = lax.bitwise_and(cell, 31) + HALO1 - 1
        near = (
            (spot_row >= cell_row)
            & (spot_row <= cell_row + 2)
            & (spot_col >= cell_col)
            & (spot_col <= cell_col + 2)
        )
        near_mask = jnp.where(near, 0.0, NEG).astype(F32)
        for h in range(HEADS):
            g = h // 4
            scores = (
                jnp.dot(
                    end_heads[h],
                    probe_query[256 * g : 256 * g + 256, pl.ds(at, 256)],
                    preferred_element_type=F32,
                )
                + near_mask
            )
            top = jnp.max(scores, axis=0, keepdims=True)
            weight = jnp.exp2((scores - top) * SCALE)
            total = jnp.sum(weight, axis=0, keepdims=True)
            mixed = jnp.dot(
                end_turned[64 * h : 64 * h + 64], weight.astype(BF), preferred_element_type=F32
            )
            mixed_ref[64 * h : 64 * h + 64] = (mixed / total).astype(BF)
        decoded = jnp.dot(head_turned[0:8], mixed_ref[...], preferred_element_type=F32)
        slot = lax.broadcasted_iota(jnp.int32, (8, 256), 1) + at
        probe_ref[:, pl.ds(at, 256)] = jnp.where(slot < live, decoded, 0.0)[0:CH]
        return carry

    lax.fori_loop(0, 4, decode, 0)


def run_prep(x0, xq, gain, perm):
    return pl.pallas_call(
        prep_kernel,
        out_shape=(
            jax.ShapeDtypeStruct((N_KEY0, WIDTH), BF),
            jax.ShapeDtypeStruct((N_MID, WIDTH), BF),
        ),
        in_specs=[pl.BlockSpec(memory_space=pltpu.VMEM)] * 4,
        out_specs=(pl.BlockSpec(memory_space=pltpu.VMEM),) * 2,
        compiler_params=pltpu.CompilerParams(vmem_limit_bytes=24 * 1024 * 1024),
        cost_estimate=pl.CostEstimate(
            flops=2 * (N_KEY0 + N_MID) * WIDTH * WIDTH, bytes_accessed=6_000_000, transcendentals=0
        ),
        name="prep",
    )(x0, xq, gain, perm)


def run_main(place, nk, nq, xq, n0, n1, gain, feat, cell, perm, pick, pieces):
    vmem = pl.BlockSpec(memory_space=pltpu.VMEM)
    return pl.pallas_call(
        main_kernel,
        out_shape=(
            jax.ShapeDtypeStruct((ROWS * COLS, WIDTH), BF),
            jax.ShapeDtypeStruct((CH, cell.shape[1]), F32),
        ),
        in_specs=[pl.BlockSpec(memory_space=pltpu.SMEM)]
        + [vmem] * 10
        + [pl.BlockSpec(memory_space=pl.ANY)] * 10,
        out_specs=(vmem, vmem),
        scratch_shapes=[
            pltpu.VMEM((2, WIDTH, HALF), BF),
            pltpu.VMEM((N_KEY0, WIDTH), BF),
            pltpu.VMEM((N_KEY0, WIDTH), BF),
            pltpu.VMEM((N_MID, WIDTH), BF),
            pltpu.VMEM((256, WIDTH), F32),
            pltpu.VMEM((N_MID, WIDTH), BF),
            pltpu.VMEM((N_MID, WIDTH), BF),
            pltpu.VMEM((N_MID, WIDTH), F32),
            pltpu.VMEM((N_MID, WIDTH), BF),
            pltpu.VMEM((256, WIDTH), F32),
            pltpu.VMEM((HEADS, 256, 256), BF),
            pltpu.VMEM((WIDTH, 256), BF),
            pltpu.VMEM((WIDTH, cell.shape[1]), BF),
            pltpu.VMEM((WIDTH, 256), BF),
            pltpu.SemaphoreType.DMA((10,)),
        ],
        compiler_params=pltpu.CompilerParams(vmem_limit_bytes=52 * 1024 * 1024),
        cost_estimate=pl.CostEstimate(
            flops=16_000_000_000, bytes_accessed=14_000_000, transcendentals=6_000_000
        ),
        name="denoise_decode",
    )(place, nk, nq, xq, n0, n1, gain, feat, cell, perm, pick, *pieces)


def features_of(offsets):
    row = np.arange(FQ)
    index = (row % 32) * 4 + row // 32
    kind = index // (FQ // 4)
    freq = (index % (FQ // 4) + 1).astype(np.float32)
    use_y = jnp.asarray((kind >= 2)[:, None])
    shift = jnp.asarray(np.where(kind % 2 == 1, math.pi / 2, 0.0).astype(np.float32)[:, None])
    position = jnp.where(use_y, offsets[1][None, :], offsets[0][None, :])
    cycles = position * jnp.asarray(freq[:, None])
    cycles = cycles - jnp.round(cycles)
    return jnp.sin(2.0 * math.pi * cycles + shift).astype(BF)


def ring(size, shift):
    return [(i, (i + shift) % size) for i in range(size)]


def halo(latents, noise):
    axes = ("gx", "pa")
    size = lax.axis_size(axes)
    n0, n1 = noise[0], noise[1]
    base = jnp.concatenate([n1[:1], latents, n0, n1[ROWS - 1 :]], axis=0)
    from_low = lax.ppermute(base[1:], axes, ring(size, 1))
    from_high = lax.ppermute(base[:-1], axes, ring(size, -1))
    far_low = lax.ppermute(latents[1:], axes, ring(size, 2))
    far_high = lax.ppermute(latents[: ROWS - 1], axes, ring(size, -2))
    lat = jnp.concatenate(
        [far_low, from_low[:ROWS], latents, from_high[1 : ROWS + 1], far_high], axis=0
    )
    first = jnp.concatenate(
        [from_low[ROWS : 2 * ROWS], n0, from_high[ROWS + 1 :]], axis=0
    )
    second = jnp.concatenate([from_low[2 * ROWS :], n1, from_high[:1]], axis=0)
    parts = ((lat, HALO0), (first, HALO1), (second, 1))
    cols = lax.axis_size("gy")

    def sent(high):
        return jnp.concatenate(
            [
                (a[:, COLS - d :] if high else a[:, :d]).reshape(-1, WIDTH)
                for a, d in parts
            ],
            axis=0,
        )

    left = lax.ppermute(sent(True), "gy", ring(cols, 1))
    right = lax.ppermute(sent(False), "gy", ring(cols, -1))
    outs = []
    at = 0
    for (a, d), pitch, lead in zip(parts, (PITCH0, PITCH1, PITCH1), (0, 0, RAD)):
        count = a.shape[0] * d
        l = left[at : at + count].reshape(a.shape[0], d, WIDTH)
        r = right[at : at + count].reshape(a.shape[0], d, WIDTH)
        at += count
        full = jnp.concatenate([l, a, r], axis=1)
        full = jnp.pad(full, ((0, 0), (lead, pitch - lead - full.shape[1]), (0, 0)))
        outs.append(full)
    x0, n0_ext, n1_ext = outs
    xq = x0[RAD : RAD + MID_ROWS, RAD : RAD + PITCH1]
    return (
        x0.reshape(N_KEY0, WIDTH),
        xq.reshape(N_MID, WIDTH),
        n0_ext.reshape(N_MID, WIDTH),
        n1_ext.reshape(N_END, WIDTH),
    )


def gather_weights(w_qkv, w_out, w_query, w_head, core):
    pack = jnp.concatenate(
        [
            w_qkv[:, WIDTH:],
            jnp.pad(w_head, ((0, 0), (0, 128 - CH))),
            w_qkv[:, :WIDTH],
            w_out,
            w_query.reshape(6, 128),
        ],
        axis=1,
    )
    mine = lax.dynamic_slice_in_dim(pack, core * HALF, HALF, 1)
    count = lax.axis_size("gx")
    block = lax.all_to_all(jnp.broadcast_to(mine[None], (count,) + mine.shape), "gx", 0, 0)
    block = block.reshape(192, HALF)
    swap = [(0, 1), (1, 0), (2, 3), (3, 2)]
    low = lax.ppermute(block, "pa", ring(4, 1))
    high = lax.ppermute(block, "pa", ring(4, -1))
    top = lax.ppermute(low[:96], "pa", ring(4, 1))
    bot = lax.ppermute(high[96:], "pa", ring(4, -1))
    mine_all = [block, low, high, top, bot]
    return mine_all + [lax.ppermute(a, "gy", swap) for a in mine_all]


def local(
    latents, noise, proc_gain, w_qkv, w_out, w_query, w_head, probe_cell, probe_offset, probe_count
):
    core = lax.rem(lax.axis_index("gy"), 2)
    place = jnp.stack([lax.axis_index("pa"), core, probe_count[0]]).astype(jnp.int32)
    x0, xq, n0, n1 = halo(latents, noise)
    pieces = gather_weights(w_qkv, w_out, w_query, w_head, core)
    perm_table, pick_table = permutation_tables()
    perm, pick = jnp.asarray(perm_table, BF), jnp.asarray(pick_table, BF)
    gain = proc_gain[None, :]
    feat = features_of(probe_offset)
    nk, nq = run_prep(x0, xq, gain, perm)
    latent, probes = run_main(
        place, nk, nq, xq, n0, n1, gain, feat, probe_cell[None, :], perm, pick, pieces
    )
    return latent.reshape(latents.shape), probes


def solution(mesh):
    return jax.shard_map(
        local,
        mesh=mesh,
        in_specs=(
            P(("gx", "pa"), "gy", None),
            P(None, ("gx", "pa"), "gy", None),
            P(),
            P(("gx", "pa"), None),
            P(("gx", "pa"), None),
            P(("gx", "pa"), None),
            P(("gx", "pa"), None),
            P(("gx", "gy", "pa")),
            P(None, ("gx", "gy", "pa")),
            P(("gx", "gy", "pa")),
        ),
        out_specs=(P(("gx", "pa"), "gy", None), P(None, ("gx", "gy", "pa"))),
        check_vma=False,
    )
```

```python
import math

import jax
import jax.numpy as jnp
import numpy as np
from jax import lax
from jax.experimental import pallas as pl
from jax.experimental.pallas import tpu as pltpu
from jax.sharding import PartitionSpec as P

HEADS = 12
FQ = 128
CH = 3
RAD = 3
STEPS = 2
EPS = 1e-06
NOISE_COEF = 0.3

WIDTH = 768
ROWS = 4
COLS = 32
HALO0 = 2 * RAD + 1
HALO1 = RAD + 1
KEY_ROWS = ROWS + 2 * HALO0
EDGE = 8
PITCH0 = COLS + 2 * EDGE
N_EDGE = EDGE * (KEY_ROWS + ROWS + 2 * HALO1 + ROWS + 2)
MID_ROWS = ROWS + 2 * HALO1
PITCH1 = COLS + 2 * HALO1
END_ROWS = ROWS + 2
N_KEY0 = KEY_ROWS * PITCH0
N_MID = MID_ROWS * PITCH1
N_END = END_ROWS * PITCH1
PAIR = 2 * PITCH1
KEYS = 384
A_HALF = 1152
B_HALF = 512
N_PAD = 544
BLOCK = 128
SWAP = [(0, 1), (1, 0), (2, 3), (3, 2)]
NEG = -1e30
SCALE = math.log2(math.e) / 8.0

BF = jnp.bfloat16
F32 = jnp.float32


def permutation_tables():
    target = np.arange(WIDTH)
    lane, rest = target // 192, target % 192
    source = (rest // 6) * 24 + lane * 6 + rest % 6
    perm = np.zeros((WIDTH, WIDTH), np.float32)
    perm[source, target] = 1.0
    pick = np.zeros((WIDTH, WIDTH), np.float32)
    out = np.arange(WIDTH)
    pick[out, (out % 128) * 6 + out // 128] = 1.0
    return perm, pick


def rms(values, gain):
    factor = lax.rsqrt(jnp.mean(values * values, axis=-1, keepdims=True) + EPS)
    return (values * factor * gain).astype(BF)


def row_lists(far_low, low, own, noise, high, far_high):
    lat = [far_low[r] for r in range(RAD)] + [low[r] for r in range(ROWS)]
    lat += [own[r] for r in range(ROWS)] + [high[1 + r] for r in range(ROWS)]
    lat += [far_high[r] for r in range(RAD)]
    first = [low[ROWS + r] for r in range(ROWS)] + [noise[0, r] for r in range(ROWS)]
    first += [high[1 + ROWS + r] for r in range(ROWS)]
    second = [low[2 * ROWS]] + [noise[1, r] for r in range(ROWS)] + [high[0]]
    return lat, first, second


def pack_kernel(far_low, low, own, noise, high, far_high, to_high, to_low, high_wide, low_wide):
    lists = row_lists(far_low, low, own, noise, high, far_high)
    for i, row in enumerate(lists[0] + lists[1] + lists[2]):
        wide = row.astype(F32)
        high_wide[EDGE * i : EDGE * i + EDGE] = wide[COLS - EDGE :]
        low_wide[EDGE * i : EDGE * i + EDGE] = wide[:EDGE]
    to_high[...] = high_wide[...].astype(BF)
    to_low[...] = low_wide[...].astype(BF)


def prep_kernel(
    far_low,
    low,
    own,
    noise,
    high,
    far_high,
    left_ref,
    right_ref,
    gain_ref,
    perm_ref,
    nk_ref,
    nq_ref,
    base_ref,
    tail_ref,
    left,
    right,
    normed_keys,
    normed_queries,
):
    gain = gain_ref[...]
    lists = row_lists(far_low, low, own, noise, high, far_high)
    left[...] = left_ref[...].astype(F32)
    right[...] = right_ref[...].astype(F32)
    cut = slice(EDGE - HALO1, EDGE + COLS + HALO1)

    def full(i, row):
        span = slice(EDGE * i, EDGE * i + EDGE)
        return jnp.concatenate([left[span], row.astype(F32), right[span]], axis=0)

    for r in range(KEY_ROWS):
        values = full(r, lists[0][r])
        normed = rms(values, gain)
        normed_keys[PITCH0 * r : PITCH0 * r + PITCH0] = normed
        m = r - RAD
        if 0 <= m < MID_ROWS:
            at = slice(PITCH1 * m, PITCH1 * m + PITCH1)
            normed_queries[at] = normed.astype(F32)[cut]
            fresh = full(KEY_ROWS + m, lists[1][m])
            base_ref[at] = (values + NOISE_COEF * fresh)[cut]
    for m in range(END_ROWS):
        fresh = full(KEY_ROWS + MID_ROWS + m, lists[2][m])
        tail_ref[PITCH1 * m : PITCH1 * m + PITCH1] = (NOISE_COEF * fresh)[cut]
    perm = perm_ref[...]
    nk_ref[...] = jnp.dot(normed_keys[...], perm, preferred_element_type=F32).astype(BF)
    nq_ref[...] = jnp.dot(
        normed_queries[...].astype(BF), perm, preferred_element_type=F32
    ).astype(BF)


def stair(index, step, count):
    total = jnp.zeros(index.shape, jnp.int32)
    for i in range(1, count):
        total = total + (index >= step * i).astype(jnp.int32)
    return total


def window_mask(pitch, rows_of_keys):
    row = lax.broadcasted_iota(jnp.int32, (PAIR, KEYS), 0)
    lane = lax.broadcasted_iota(jnp.int32, (PAIR, KEYS), 1)
    q_row = stair(row, PITCH1, 2)
    q_col = row - PITCH1 * q_row
    k_row = stair(lane, pitch, rows_of_keys)
    k_col = lane - pitch * k_row
    return q_row, q_col, k_row, k_col


def attend(queries, keys, values, mask):
    rows = queries.shape[0]
    lane_head = stair(lax.broadcasted_iota(jnp.int32, (rows, 256), 1), 64, 4)
    zero = jnp.zeros((), BF)
    stacked = jnp.concatenate(
        [jnp.where(lane_head == h, queries, zero) for h in range(4)], axis=0
    )
    scores = lax.dot_general(
        stacked, keys, (((1,), (1,)), ((), ())), preferred_element_type=F32
    )
    parts = []
    for h in range(4):
        part = scores[h * rows : (h + 1) * rows] + mask
        top = jnp.max(part, axis=1, keepdims=True)
        weight = jnp.exp2(part - top)
        total = jnp.sum(weight, axis=1, keepdims=True)
        parts.append((weight.astype(BF), 1.0 / total))
    mixed = jnp.dot(
        jnp.concatenate([p[0] for p in parts], axis=0), values, preferred_element_type=F32
    )
    result = mixed[0:rows] * parts[0][1]
    for h in range(1, 4):
        result = jnp.where(
            lane_head == h, mixed[h * rows : (h + 1) * rows] * parts[h][1], result
        )
    return result.astype(BF)


def start_copies(core, pieces, target, sems, width):
    def copy_of(slot, ref, at):
        start = pl.multiple_of(at * width, 128)
        return pltpu.make_async_copy(ref, target.at[:, pl.ds(start, width)], sems.at[slot])

    copy_of(0, pieces[0], core).start()
    copy_of(1, pieces[1], 1 - core).start()

    def wait():
        copy_of(0, pieces[0], core).wait()
        copy_of(1, pieces[1], 1 - core).wait()

    return wait


def project(source, weights, column, target, rows, scale=None):
    for t in range(0, WIDTH, 256):
        product = jnp.dot(
            source[...],
            weights[:, column + t : column + t + 256],
            preferred_element_type=F32,
        )
        if scale is not None:
            product = product * scale
        target[0:rows, t : t + 256] = product.astype(BF).astype(target.dtype)


def first_kernel(
    place_ref, nk_ref, nq_ref, perm_ref, mine, other, att_ref, weights, keys, values, queries, att, sems
):
    wait = start_copies(place_ref[0], (mine, other), weights, sems, A_HALF)
    q_row, q_col, k_row, k_col = window_mask(PITCH0, 8)
    inside = (
        (k_row >= q_row)
        & (k_row <= q_row + 2 * RAD)
        & (k_col >= q_col + EDGE - HALO1 - RAD)
        & (k_col <= q_col + EDGE - HALO1 + RAD)
    )
    mask = jnp.where(inside, 0.0, NEG).astype(F32)
    wait()
    project(nk_ref, weights, 0, keys, N_KEY0)
    project(nk_ref, weights, WIDTH, values, N_KEY0)
    project(nq_ref, weights, 2 * WIDTH, queries, N_MID, SCALE)

    def attend0(j, carry):
        q_at = pl.multiple_of(j * PAIR, PAIR)
        k_at = pl.multiple_of(j * 2 * PITCH0, 2 * PITCH0)
        for g in range(3):
            cols = slice(256 * g, 256 * g + 256)
            att[pl.ds(q_at, PAIR), cols] = attend(
                queries[pl.ds(q_at, PAIR), cols],
                keys[pl.ds(k_at, KEYS), cols],
                values[pl.ds(k_at, KEYS), cols],
                mask,
            )
        return carry

    lax.fori_loop(0, MID_ROWS // 2, attend0, 0)
    att_ref[...] = jnp.dot(
        att[...], perm_ref[...], preferred_element_type=F32
    ).astype(BF)


def second_kernel(
    place_ref,
    att0_ref,
    base_ref,
    noise_ref,
    gain_ref,
    feat_ref,
    cell_ref,
    perm_ref,
    pick_ref,
    mine_a,
    other_a,
    mine_b,
    other_b,
    latent_ref,
    probe_ref,
    weights,
    tail,
    keys,
    values,
    queries,
    att,
    att_perm,
    lat_mid,
    mid_perm,
    lat_end,
    end_low,
    probe_query,
    sems_a,
    sems_b,
):
    live = place_ref[1]
    wait_b = start_copies(place_ref[0], (mine_b, other_b), tail, sems_b, B_HALF)
    wait_a = start_copies(place_ref[0], (mine_a, other_a), weights, sems_a, A_HALF)
    wait_b()

    for t in range(3):
        cols = slice(256 * t, 256 * t + 256)
        update = jnp.dot(att0_ref[...], tail[:, cols], preferred_element_type=F32)
        fresh = base_ref[:, cols] + update / STEPS
        lat_mid[:, cols] = fresh.astype(BF).astype(F32)

    mid_perm[...] = jnp.dot(
        rms(lat_mid[...], gain_ref[...]), perm_ref[...], preferred_element_type=F32
    ).astype(BF)
    keys[N_MID:] = jnp.zeros((N_PAD - N_MID, WIDTH), BF)
    values[N_MID:] = jnp.zeros((N_PAD - N_MID, WIDTH), BF)
    wait_a()
    project(mid_perm, weights, 0, keys, N_MID)
    project(mid_perm, weights, WIDTH, values, N_MID)
    project(mid_perm.at[112:368], weights, 2 * WIDTH, queries, 256, SCALE)

    q_row, q_col, k_row, k_col = window_mask(PITCH1, 10)
    inside = (
        (k_row >= q_row)
        & (k_row <= q_row + 2 * RAD)
        & (k_col >= q_col - RAD)
        & (k_col <= q_col + RAD)
    )
    mask = jnp.where(inside, 0.0, NEG).astype(F32)

    def attend1(j, carry):
        at = pl.multiple_of(j * PAIR, PAIR)
        for g in range(3):
            cols = slice(256 * g, 256 * g + 256)
            att[pl.ds(at, PAIR), cols] = attend(
                queries[pl.ds(pl.multiple_of(at + 8, 8), PAIR), cols].astype(BF),
                keys[pl.ds(at, KEYS), cols],
                values[pl.ds(at, KEYS), cols],
                mask,
            )
        return carry

    lax.fori_loop(0, END_ROWS // 2, attend1, 0)
    att_perm[...] = jnp.dot(att[...], perm_ref[...], preferred_element_type=F32).astype(BF)

    lat_end[N_END:] = jnp.zeros((256 - N_END, WIDTH), F32)
    for t in range(3):
        cols = slice(256 * t, 256 * t + 256)
        update = jnp.dot(att_perm[...], tail[:, cols], preferred_element_type=F32)
        fresh = (
            lat_mid[RAD * PITCH1 : RAD * PITCH1 + N_END, cols]
            + update / STEPS
            + noise_ref[:, cols]
        )
        lat_end[0:N_END, cols] = fresh.astype(BF).astype(F32)
    for r in range(ROWS):
        start = PITCH1 * (r + 1) + HALO1
        latent_ref[COLS * r : COLS * r + COLS] = lat_end[start : start + COLS].astype(BF)

    end_low[...] = lat_end[...].astype(BF)
    query_rows = jnp.dot(
        pick_ref[...], tail[:, 768:896], preferred_element_type=F32
    ).astype(BF)
    for i in range(6):
        probe_query[:, 128 * i : 128 * i + 128] = (
            jnp.dot(
                feat_ref[...], query_rows[128 * i : 128 * i + 128], preferred_element_type=F32
            )
            * SCALE
        ).astype(BF)
    head_rows = jnp.dot(perm_ref[...], tail[:, 896:1024], preferred_element_type=F32)
    head_turned = head_rows.T[0:8].astype(BF)

    spot = lax.broadcasted_iota(jnp.int32, (BLOCK, 256), 1)
    spot_row = stair(spot, PITCH1, 7)
    spot_col = spot - PITCH1 * spot_row

    def decode(b, carry):
        at = pl.multiple_of(b * BLOCK, BLOCK)
        cell = cell_ref[pl.ds(at, BLOCK)]
        cell_row = lax.shift_right_logical(cell, 5)
        cell_col = lax.bitwise_and(cell, 31) + HALO1 - 1
        near = (
            (spot_row >= cell_row)
            & (spot_row <= cell_row + 2)
            & (spot_col >= cell_col)
            & (spot_col <= cell_col + 2)
        )
        near_mask = jnp.where(near, 0.0, NEG).astype(F32)
        mixed = []
        for g in range(3):
            cols = slice(256 * g, 256 * g + 256)
            mixed.append(
                attend(
                    probe_query[pl.ds(at, BLOCK), cols], end_low[:, cols], end_low[:, cols], near_mask
                )
            )
        decoded = lax.dot_general(
            head_turned,
            jnp.concatenate(mixed, axis=1),
            (((1,), (1,)), ((), ())),
            preferred_element_type=F32,
        )
        slot = lax.broadcasted_iota(jnp.int32, (8, BLOCK), 1) + at
        probe_ref[:, pl.ds(at, BLOCK)] = jnp.where(slot < live, decoded, 0.0)[0:CH]
        return carry

    lax.fori_loop(0, feat_ref.shape[0] // BLOCK, decode, 0)


def run_pack(rows):
    vmem = pl.BlockSpec(memory_space=pltpu.VMEM)
    return pl.pallas_call(
        pack_kernel,
        out_shape=(jax.ShapeDtypeStruct((N_EDGE, WIDTH), BF),) * 2,
        in_specs=[vmem] * 6,
        out_specs=(vmem,) * 2,
        scratch_shapes=[pltpu.VMEM((N_EDGE, WIDTH), F32)] * 2,
        compiler_params=pltpu.CompilerParams(vmem_limit_bytes=12 * 1024 * 1024),
        cost_estimate=pl.CostEstimate(flops=0, bytes_accessed=3_000_000, transcendentals=0),
        name="pack",
    )(*rows)


def run_prep(rows, left, right, gain, perm):
    vmem = pl.BlockSpec(memory_space=pltpu.VMEM)
    return pl.pallas_call(
        prep_kernel,
        out_shape=(
            jax.ShapeDtypeStruct((N_KEY0, WIDTH), BF),
            jax.ShapeDtypeStruct((N_MID, WIDTH), BF),
            jax.ShapeDtypeStruct((N_MID, WIDTH), F32),
            jax.ShapeDtypeStruct((N_END, WIDTH), F32),
        ),
        in_specs=[vmem] * 10,
        out_specs=(vmem,) * 4,
        scratch_shapes=[
            pltpu.VMEM((N_EDGE, WIDTH), F32),
            pltpu.VMEM((N_EDGE, WIDTH), F32),
            pltpu.VMEM((N_KEY0, WIDTH), BF),
            pltpu.VMEM((N_MID, WIDTH), F32),
        ],
        compiler_params=pltpu.CompilerParams(vmem_limit_bytes=20 * 1024 * 1024),
        cost_estimate=pl.CostEstimate(
            flops=2 * (N_KEY0 + N_MID) * WIDTH * WIDTH, bytes_accessed=8_000_000, transcendentals=0
        ),
        name="prep",
    )(*rows, left, right, gain, perm)


def run_first(place, nk, nq, perm, mine, other):
    vmem = pl.BlockSpec(memory_space=pltpu.VMEM)
    anywhere = pl.BlockSpec(memory_space=pl.ANY)
    return pl.pallas_call(
        first_kernel,
        out_shape=jax.ShapeDtypeStruct((N_MID, WIDTH), BF),
        in_specs=[pl.BlockSpec(memory_space=pltpu.SMEM), vmem, vmem, vmem, anywhere, anywhere],
        out_specs=vmem,
        scratch_shapes=[
            pltpu.VMEM((WIDTH, 3 * WIDTH), BF),
            pltpu.VMEM((N_KEY0, WIDTH), BF),
            pltpu.VMEM((N_KEY0, WIDTH), BF),
            pltpu.VMEM((N_MID, WIDTH), BF),
            pltpu.VMEM((N_MID, WIDTH), BF),
            pltpu.SemaphoreType.DMA((2,)),
        ],
        compiler_params=pltpu.CompilerParams(vmem_limit_bytes=22 * 1024 * 1024),
        cost_estimate=pl.CostEstimate(
            flops=8_000_000_000, bytes_accessed=8_000_000, transcendentals=2_500_000
        ),
        name="first_step",
    )(place, nk, nq, perm, mine, other)


def run_second(place, att, base, noise, gain, feat, cell, perm, pick, pieces):
    vmem = pl.BlockSpec(memory_space=pltpu.VMEM)
    return pl.pallas_call(
        second_kernel,
        out_shape=(
            jax.ShapeDtypeStruct((ROWS * COLS, WIDTH), BF),
            jax.ShapeDtypeStruct((CH, cell.shape[0]), F32),
        ),
        in_specs=[pl.BlockSpec(memory_space=pltpu.SMEM)]
        + [vmem] * 8
        + [pl.BlockSpec(memory_space=pl.ANY)] * 4,
        out_specs=(vmem, vmem),
        scratch_shapes=[
            pltpu.VMEM((WIDTH, 3 * WIDTH), BF),
            pltpu.VMEM((WIDTH, 2 * B_HALF), BF),
            pltpu.VMEM((N_PAD, WIDTH), BF),
            pltpu.VMEM((N_PAD, WIDTH), BF),
            pltpu.VMEM((256, WIDTH), F32),
            pltpu.VMEM((N_END, WIDTH), BF),
            pltpu.VMEM((N_END, WIDTH), BF),
            pltpu.VMEM((N_MID, WIDTH), F32),
            pltpu.VMEM((N_MID, WIDTH), BF),
            pltpu.VMEM((256, WIDTH), F32),
            pltpu.VMEM((256, WIDTH), BF),
            pltpu.VMEM((cell.shape[0], WIDTH), BF),
            pltpu.SemaphoreType.DMA((2,)),
            pltpu.SemaphoreType.DMA((2,)),
        ],
        compiler_params=pltpu.CompilerParams(vmem_limit_bytes=26 * 1024 * 1024),
        cost_estimate=pl.CostEstimate(
            flops=8_000_000_000, bytes_accessed=14_000_000, transcendentals=4_500_000
        ),
        name="second_step",
    )(place, att, base, noise, gain, feat, cell, perm, pick, *pieces)


def features_of(offsets):
    row = np.arange(FQ)
    index = (row % 32) * 4 + row // 32
    kind = index // (FQ // 4)
    freq = (index % (FQ // 4) + 1).astype(np.float32)
    use_y = jnp.asarray((kind >= 2)[None, :])
    shift = jnp.asarray(np.where(kind % 2 == 1, math.pi / 2, 0.0).astype(np.float32)[None, :])
    position = jnp.where(use_y, offsets[1][:, None], offsets[0][:, None])
    cycles = position * jnp.asarray(freq[None, :])
    cycles = cycles - jnp.round(cycles)
    return jnp.sin(2.0 * math.pi * cycles + shift).astype(BF)


def ring(size, shift):
    return [(i, (i + shift) % size) for i in range(size)]


def halo_rows(latents, noise):
    axes = ("gx", "pa")
    size = lax.axis_size(axes)
    n0, n1 = noise[0], noise[1]
    base = jnp.concatenate([n1[:1], latents, n0, n1[ROWS - 1 :]], axis=0)
    return (
        lax.ppermute(latents[1:], axes, ring(size, 2)),
        lax.ppermute(base[1:], axes, ring(size, 1)),
        latents,
        noise,
        lax.ppermute(base[:-1], axes, ring(size, -1)),
        lax.ppermute(latents[:RAD], axes, ring(size, -2)),
    )


def pack_weights(w_qkv, w_out, w_query, w_head, core):
    head = [w_qkv[:, WIDTH:], w_qkv[:, :WIDTH]]
    tail = [w_out, w_query.reshape(6, 128), jnp.pad(w_head, ((0, 0), (0, 128 - CH)))]
    a = jnp.concatenate(head, axis=1)
    b = jnp.concatenate(tail, axis=1)
    mine = jnp.concatenate(
        [
            lax.dynamic_slice_in_dim(a, core * A_HALF, A_HALF, 1),
            lax.dynamic_slice_in_dim(b, core * B_HALF, B_HALF, 1),
        ],
        axis=1,
    )
    return jnp.broadcast_to(mine[None], (lax.axis_size("gx"),) + mine.shape)


def gather_long(shares):
    return lax.all_to_all(shares, "gx", 0, 0).reshape(192, A_HALF + B_HALF)


def gather_short(block):
    count = lax.axis_size("pa")
    wide = lax.all_to_all(jnp.broadcast_to(block[None], (count,) + block.shape), "pa", 0, 0)
    return wide.reshape(WIDTH, block.shape[1])


def local(
    latents, noise, proc_gain, w_qkv, w_out, w_query, w_head, probe_cell, probe_offset, probe_count
):
    barrier = lax.optimization_barrier
    cols = lax.axis_size("gy")
    perm_table, pick_table = permutation_tables()
    perm, pick = jnp.asarray(perm_table, BF), jnp.asarray(pick_table, BF)
    gain = proc_gain[None, :]
    core = lax.rem(lax.axis_index("gy"), 2)
    place = jnp.stack([core, probe_count[0]]).astype(jnp.int32)

    shares = pack_weights(w_qkv, w_out, w_query, w_head, core)
    shares, latents, noise = barrier((shares, latents, noise))
    rows = halo_rows(latents, noise)
    block, rows = barrier((gather_long(shares), rows))
    wide_a = gather_short(block[:, :A_HALF])
    to_high, to_low = run_pack(rows)
    left = lax.ppermute(to_high, "gy", ring(cols, 1))
    right = lax.ppermute(to_low, "gy", ring(cols, -1))
    nk, nq, base, tail_noise = run_prep(rows, left, right, gain, perm)
    feat = features_of(probe_offset)
    cell = probe_cell[:, None]
    wide_a, nk, nq, base, tail_noise, feat, cell, block = barrier(
        (wide_a, nk, nq, base, tail_noise, feat, cell, block)
    )
    other_a = lax.ppermute(wide_a, "gy", SWAP)
    wide_b = gather_short(block[:, A_HALF:])
    att = run_first(place, nk, nq, perm, wide_a, other_a)
    wide_b, att = barrier((wide_b, att))
    other_b = lax.ppermute(wide_b, "gy", SWAP)
    latent, probes = run_second(
        place, att, base, tail_noise, gain, feat, cell, perm, pick,
        (wide_a, other_a, wide_b, other_b),
    )
    return latent.reshape(latents.shape), probes


def solution(mesh):
    return jax.shard_map(
        local,
        mesh=mesh,
        in_specs=(
            P(("gx", "pa"), "gy", None),
            P(None, ("gx", "pa"), "gy", None),
            P(),
            P(("gx", "pa"), None),
            P(("gx", "pa"), None),
            P(("gx", "pa"), None),
            P(("gx", "pa"), None),
            P(("gx", "gy", "pa")),
            P(None, ("gx", "gy", "pa")),
            P(("gx", "gy", "pa")),
        ),
        out_specs=(P(("gx", "pa"), "gy", None), P(None, ("gx", "gy", "pa"))),
        check_vma=False,
    )
```

```python
import math

import jax
import jax.numpy as jnp
import numpy as np
from jax import lax
from jax.experimental import pallas as pl
from jax.experimental.pallas import tpu as pltpu
from jax.sharding import PartitionSpec as P

HEADS = 12
FQ = 128
CH = 3
RAD = 3
STEPS = 2
EPS = 1e-06
NOISE_COEF = 0.3

WIDTH = 768
ROWS = 4
COLS = 32
HALO0 = 2 * RAD + 1
HALO1 = RAD + 1
KEY_ROWS = ROWS + 2 * HALO0
EDGE = 8
PITCH0 = COLS + 2 * EDGE
N_EDGE = EDGE * (KEY_ROWS + ROWS + 2 * HALO1 + ROWS + 2)
MID_ROWS = ROWS + 2 * HALO1
PITCH1 = COLS + 2 * HALO1
END_ROWS = ROWS + 2
N_KEY0 = KEY_ROWS * PITCH0
N_MID = MID_ROWS * PITCH1
N_END = END_ROWS * PITCH1
PAIR = 2 * PITCH1
KEYS = 384
HALF = 1664
TAIL = 3 * WIDTH
BLOCK = 128
SWAP = [(0, 1), (1, 0), (2, 3), (3, 2)]
NEG = -1e30
SCALE = math.log2(math.e) / 8.0

BF = jnp.bfloat16
F32 = jnp.float32


def permutation_tables():
    target = np.arange(WIDTH)
    lane, rest = target // 192, target % 192
    source = (rest // 6) * 24 + lane * 6 + rest % 6
    perm = np.zeros((WIDTH, WIDTH), np.float32)
    perm[source, target] = 1.0
    pick = np.zeros((WIDTH, WIDTH), np.float32)
    out = np.arange(WIDTH)
    pick[out, (out % 128) * 6 + out // 128] = 1.0
    return perm, pick


def rms(values, gain):
    factor = lax.rsqrt(jnp.mean(values * values, axis=-1, keepdims=True) + EPS)
    return (values * factor * gain).astype(BF)


def row_lists(far_low, low, own, noise, high, far_high):
    lat = [far_low[r] for r in range(RAD)] + [low[r] for r in range(ROWS)]
    lat += [own[r] for r in range(ROWS)] + [high[1 + r] for r in range(ROWS)]
    lat += [far_high[r] for r in range(RAD)]
    first = [low[ROWS + r] for r in range(ROWS)] + [noise[0, r] for r in range(ROWS)]
    first += [high[1 + ROWS + r] for r in range(ROWS)]
    second = [low[2 * ROWS]] + [noise[1, r] for r in range(ROWS)] + [high[0]]
    return lat, first, second


def pack_kernel(far_low, low, own, noise, high, far_high, to_high, to_low, high_wide, low_wide):
    lists = row_lists(far_low, low, own, noise, high, far_high)
    for i, row in enumerate(lists[0] + lists[1] + lists[2]):
        wide = row.astype(F32)
        high_wide[EDGE * i : EDGE * i + EDGE] = wide[COLS - EDGE :]
        low_wide[EDGE * i : EDGE * i + EDGE] = wide[:EDGE]
    to_high[...] = high_wide[...].astype(BF)
    to_low[...] = low_wide[...].astype(BF)


def prep_kernel(
    far_low,
    low,
    own,
    noise,
    high,
    far_high,
    left_ref,
    right_ref,
    gain_ref,
    perm_ref,
    nk_ref,
    nq_ref,
    base_ref,
    tail_ref,
    left,
    right,
    normed_keys,
    normed_queries,
):
    gain = gain_ref[...]
    lists = row_lists(far_low, low, own, noise, high, far_high)
    left[...] = left_ref[...].astype(F32)
    right[...] = right_ref[...].astype(F32)
    cut = slice(EDGE - HALO1, EDGE + COLS + HALO1)

    def full(i, row):
        span = slice(EDGE * i, EDGE * i + EDGE)
        return jnp.concatenate([left[span], row.astype(F32), right[span]], axis=0)

    for r in range(KEY_ROWS):
        values = full(r, lists[0][r])
        normed = rms(values, gain)
        normed_keys[PITCH0 * r : PITCH0 * r + PITCH0] = normed
        m = r - RAD
        if 0 <= m < MID_ROWS:
            at = slice(PITCH1 * m, PITCH1 * m + PITCH1)
            normed_queries[at] = normed.astype(F32)[cut]
            fresh = full(KEY_ROWS + m, lists[1][m])
            base_ref[at] = (values + NOISE_COEF * fresh)[cut]
    for m in range(END_ROWS):
        fresh = full(KEY_ROWS + MID_ROWS + m, lists[2][m])
        tail_ref[PITCH1 * m : PITCH1 * m + PITCH1] = (NOISE_COEF * fresh)[cut]
    perm = perm_ref[...]
    nk_ref[...] = jnp.dot(normed_keys[...], perm, preferred_element_type=F32).astype(BF)
    nq_ref[...] = jnp.dot(
        normed_queries[...].astype(BF), perm, preferred_element_type=F32
    ).astype(BF)


def stair(index, step, count):
    total = jnp.zeros(index.shape, jnp.int32)
    for i in range(1, count):
        total = total + (index >= step * i).astype(jnp.int32)
    return total


def window_mask(pitch, rows_of_keys):
    row = lax.broadcasted_iota(jnp.int32, (PAIR, KEYS), 0)
    lane = lax.broadcasted_iota(jnp.int32, (PAIR, KEYS), 1)
    q_row = stair(row, PITCH1, 2)
    q_col = row - PITCH1 * q_row
    k_row = stair(lane, pitch, rows_of_keys)
    k_col = lane - pitch * k_row
    return q_row, q_col, k_row, k_col


def attend(queries, keys, values, mask):
    rows = queries.shape[0]
    lane_head = stair(lax.broadcasted_iota(jnp.int32, (rows, 256), 1), 64, 4)
    zero = jnp.zeros((), BF)
    stacked = jnp.concatenate(
        [jnp.where(lane_head == h, queries, zero) for h in range(4)], axis=0
    )
    scores = lax.dot_general(
        stacked, keys, (((1,), (1,)), ((), ())), preferred_element_type=F32
    )
    parts = []
    for h in range(4):
        part = scores[h * rows : (h + 1) * rows] + mask
        top = jnp.max(part, axis=1, keepdims=True)
        weight = jnp.exp2(part - top)
        total = jnp.sum(weight, axis=1, keepdims=True)
        parts.append((weight.astype(BF), 1.0 / total))
    mixed = jnp.dot(
        jnp.concatenate([p[0] for p in parts], axis=0), values, preferred_element_type=F32
    )
    result = mixed[0:rows] * parts[0][1]
    for h in range(1, 4):
        result = jnp.where(
            lane_head == h, mixed[h * rows : (h + 1) * rows] * parts[h][1], result
        )
    return result.astype(BF)


def project(source, weights, column, target, rows, scale=None):
    for t in range(0, WIDTH, 256):
        product = jnp.dot(
            source[...],
            weights[:, column + t : column + t + 256],
            preferred_element_type=F32,
        )
        if scale is not None:
            product = product * scale
        target[0:rows, t : t + 256] = product.astype(BF).astype(target.dtype)


def main_kernel(
    place_ref,
    gain_ref,
    nk_any,
    nq_any,
    base_any,
    noise_any,
    feat_any,
    cell_any,
    perm_any,
    pick_any,
    mine,
    other,
    latent_ref,
    probe_ref,
    weights,
    nk_ref,
    nq_ref,
    base_ref,
    noise_ref,
    feat_ref,
    cell_ref,
    perm_ref,
    pick_ref,
    keys,
    values,
    q_low,
    queries,
    att,
    att_perm,
    lat_mid,
    mid_perm,
    lat_end,
    end_low,
    probe_query,
    half_sems,
    sems,
):
    core = place_ref[0]
    live = place_ref[1]

    def half(ref, slot):
        start = pl.multiple_of(slot * HALF, 128)
        return pltpu.make_async_copy(
            ref, weights.at[:, pl.ds(start, HALF)], half_sems.at[slot]
        )

    pairs = (
        (nk_any, nk_ref),
        (nq_any, nq_ref),
        (perm_any, perm_ref),
        (base_any, base_ref),
        (noise_any, noise_ref),
        (pick_any, pick_ref),
        (feat_any, feat_ref),
        (cell_any, cell_ref),
    )
    loads = [pltpu.make_async_copy(a, b, sems.at[n]) for n, (a, b) in enumerate(pairs)]
    loads[0].start()
    half(mine, core).start()
    half(other, 1 - core).start()
    for load in loads[1:]:
        load.start()

    q_row, q_col, k_row, k_col = window_mask(PITCH0, 8)
    inside = (
        (k_row >= q_row)
        & (k_row <= q_row + 2 * RAD)
        & (k_col >= q_col + EDGE - HALO1 - RAD)
        & (k_col <= q_col + EDGE - HALO1 + RAD)
    )
    mask = jnp.where(inside, 0.0, NEG).astype(F32)
    loads[0].wait()
    half(mine, 0).wait()
    project(nk_ref, weights, 0, keys, N_KEY0)
    project(nk_ref, weights, WIDTH, values, N_KEY0)
    loads[1].wait()
    half(mine, 1).wait()
    project(nq_ref, weights, 2 * WIDTH, q_low, N_MID, SCALE)

    def attend0(j, carry):
        q_at = pl.multiple_of(j * PAIR, PAIR)
        k_at = pl.multiple_of(j * 2 * PITCH0, 2 * PITCH0)
        for g in range(3):
            cols = slice(256 * g, 256 * g + 256)
            att[pl.ds(q_at, PAIR), cols] = attend(
                q_low[pl.ds(q_at, PAIR), cols],
                keys[pl.ds(k_at, KEYS), cols],
                values[pl.ds(k_at, KEYS), cols],
                mask,
            )
        return carry

    lax.fori_loop(0, MID_ROWS // 2, attend0, 0)
    for load in loads[2:]:
        load.wait()
    att_perm[...] = jnp.dot(att[...], perm_ref[...], preferred_element_type=F32).astype(BF)
    for t in range(3):
        cols = slice(256 * t, 256 * t + 256)
        update = jnp.dot(
            att_perm[...],
            weights[:, TAIL + 256 * t : TAIL + 256 * t + 256],
            preferred_element_type=F32,
        )
        fresh = base_ref[:, cols] + update / STEPS
        lat_mid[:, cols] = fresh.astype(BF).astype(F32)

    mid_perm[...] = jnp.dot(
        rms(lat_mid[...], gain_ref[...]), perm_ref[...], preferred_element_type=F32
    ).astype(BF)
    project(mid_perm, weights, 0, keys, N_MID)
    project(mid_perm, weights, WIDTH, values, N_MID)
    project(mid_perm.at[112:368], weights, 2 * WIDTH, queries, 256, SCALE)

    q_row, q_col, k_row, k_col = window_mask(PITCH1, 10)
    inside = (
        (k_row >= q_row)
        & (k_row <= q_row + 2 * RAD)
        & (k_col >= q_col - RAD)
        & (k_col <= q_col + RAD)
    )
    mask = jnp.where(inside, 0.0, NEG).astype(F32)

    def attend1(j, carry):
        at = pl.multiple_of(j * PAIR, PAIR)
        for g in range(3):
            cols = slice(256 * g, 256 * g + 256)
            att[pl.ds(at, PAIR), cols] = attend(
                queries[pl.ds(pl.multiple_of(at + 8, 8), PAIR), cols].astype(BF),
                keys[pl.ds(at, KEYS), cols],
                values[pl.ds(at, KEYS), cols],
                mask,
            )
        return carry

    lax.fori_loop(0, END_ROWS // 2, attend1, 0)
    att_perm[0:N_END] = jnp.dot(
        att[0:N_END], perm_ref[...], preferred_element_type=F32
    ).astype(BF)

    lat_end[N_END:] = jnp.zeros((256 - N_END, WIDTH), F32)
    for t in range(3):
        cols = slice(256 * t, 256 * t + 256)
        update = jnp.dot(
            att_perm[0:N_END],
            weights[:, TAIL + 256 * t : TAIL + 256 * t + 256],
            preferred_element_type=F32,
        )
        fresh = (
            lat_mid[RAD * PITCH1 : RAD * PITCH1 + N_END, cols]
            + update / STEPS
            + noise_ref[:, cols]
        )
        lat_end[0:N_END, cols] = fresh.astype(BF).astype(F32)
    for r in range(ROWS):
        start = PITCH1 * (r + 1) + HALO1
        latent_ref[COLS * r : COLS * r + COLS] = lat_end[start : start + COLS].astype(BF)

    end_low[...] = lat_end[...].astype(BF)
    query_rows = jnp.dot(
        pick_ref[...], weights[:, TAIL + 768 : TAIL + 896], preferred_element_type=F32
    ).astype(BF)
    for i in range(6):
        probe_query[:, 128 * i : 128 * i + 128] = (
            jnp.dot(
                feat_ref[...], query_rows[128 * i : 128 * i + 128], preferred_element_type=F32
            )
            * SCALE
        ).astype(BF)
    head_rows = jnp.dot(perm_ref[...], weights[:, TAIL + 896 : TAIL + 1024], preferred_element_type=F32)
    head_turned = head_rows.T[0:8].astype(BF)

    spot = lax.broadcasted_iota(jnp.int32, (BLOCK, 256), 1)
    spot_row = stair(spot, PITCH1, 7)
    spot_col = spot - PITCH1 * spot_row

    def decode(b, carry):
        at = pl.multiple_of(b * BLOCK, BLOCK)
        cell = cell_ref[pl.ds(at, BLOCK)]
        cell_row = lax.shift_right_logical(cell, 5)
        cell_col = lax.bitwise_and(cell, 31) + HALO1 - 1
        near = (
            (spot_row >= cell_row)
            & (spot_row <= cell_row + 2)
            & (spot_col >= cell_col)
            & (spot_col <= cell_col + 2)
        )
        near_mask = jnp.where(near, 0.0, NEG).astype(F32)
        mixed = []
        for g in range(3):
            cols = slice(256 * g, 256 * g + 256)
            mixed.append(
                attend(
                    probe_query[pl.ds(at, BLOCK), cols], end_low[:, cols], end_low[:, cols], near_mask
                )
            )
        decoded = lax.dot_general(
            head_turned,
            jnp.concatenate(mixed, axis=1),
            (((1,), (1,)), ((), ())),
            preferred_element_type=F32,
        )
        slot = lax.broadcasted_iota(jnp.int32, (8, BLOCK), 1) + at
        probe_ref[:, pl.ds(at, BLOCK)] = jnp.where(slot < live, decoded, 0.0)[0:CH]
        return carry

    lax.fori_loop(0, feat_ref.shape[0] // BLOCK, decode, 0)


def run_pack(rows):
    vmem = pl.BlockSpec(memory_space=pltpu.VMEM)
    return pl.pallas_call(
        pack_kernel,
        out_shape=(jax.ShapeDtypeStruct((N_EDGE, WIDTH), BF),) * 2,
        in_specs=[vmem] * 6,
        out_specs=(vmem,) * 2,
        scratch_shapes=[pltpu.VMEM((N_EDGE, WIDTH), F32)] * 2,
        compiler_params=pltpu.CompilerParams(vmem_limit_bytes=60 * 1024 * 1024),
        cost_estimate=pl.CostEstimate(flops=0, bytes_accessed=3_000_000, transcendentals=0),
        name="pack",
    )(*rows)


def run_prep(rows, left, right, gain, perm):
    vmem = pl.BlockSpec(memory_space=pltpu.VMEM)
    return pl.pallas_call(
        prep_kernel,
        out_shape=(
            jax.ShapeDtypeStruct((N_KEY0, WIDTH), BF),
            jax.ShapeDtypeStruct((N_MID, WIDTH), BF),
            jax.ShapeDtypeStruct((N_MID, WIDTH), F32),
            jax.ShapeDtypeStruct((N_END, WIDTH), F32),
        ),
        in_specs=[vmem] * 10,
        out_specs=(vmem,) * 4,
        scratch_shapes=[
            pltpu.VMEM((N_EDGE, WIDTH), F32),
            pltpu.VMEM((N_EDGE, WIDTH), F32),
            pltpu.VMEM((N_KEY0, WIDTH), BF),
            pltpu.VMEM((N_MID, WIDTH), F32),
        ],
        compiler_params=pltpu.CompilerParams(vmem_limit_bytes=60 * 1024 * 1024),
        cost_estimate=pl.CostEstimate(
            flops=2 * (N_KEY0 + N_MID) * WIDTH * WIDTH, bytes_accessed=8_000_000, transcendentals=0
        ),
        name="prep",
    )(*rows, left, right, gain, perm)


def run_main(place, gain, arrays, mine, other):
    vmem = pl.BlockSpec(memory_space=pltpu.VMEM)
    probes = arrays[5].shape[0]
    return pl.pallas_call(
        main_kernel,
        out_shape=(
            jax.ShapeDtypeStruct((ROWS * COLS, WIDTH), BF),
            jax.ShapeDtypeStruct((CH, probes), F32),
        ),
        in_specs=[pl.BlockSpec(memory_space=pltpu.SMEM), vmem]
        + [pl.BlockSpec(memory_space=pl.ANY)] * (len(arrays) + 2),
        out_specs=(vmem, vmem),
        scratch_shapes=[pltpu.VMEM((WIDTH, 2 * HALF), BF)]
        + [pltpu.VMEM(a.shape, a.dtype) for a in arrays]
        + [
            pltpu.VMEM((N_KEY0, WIDTH), BF),
            pltpu.VMEM((N_KEY0, WIDTH), BF),
            pltpu.VMEM((N_MID, WIDTH), BF),
            pltpu.VMEM((256, WIDTH), F32),
            pltpu.VMEM((N_MID, WIDTH), BF),
            pltpu.VMEM((N_MID, WIDTH), BF),
            pltpu.VMEM((N_MID, WIDTH), F32),
            pltpu.VMEM((N_MID, WIDTH), BF),
            pltpu.VMEM((256, WIDTH), F32),
            pltpu.VMEM((256, WIDTH), BF),
            pltpu.VMEM((probes, WIDTH), BF),
            pltpu.SemaphoreType.DMA((2,)),
            pltpu.SemaphoreType.DMA((len(arrays),)),
        ],
        compiler_params=pltpu.CompilerParams(vmem_limit_bytes=60 * 1024 * 1024),
        cost_estimate=pl.CostEstimate(
            flops=16_000_000_000, bytes_accessed=16_000_000, transcendentals=7_000_000
        ),
        name="denoise_decode",
    )(place, gain, *arrays, mine, other)


def features_of(offsets):
    row = np.arange(FQ)
    index = (row % 32) * 4 + row // 32
    kind = index // (FQ // 4)
    freq = (index % (FQ // 4) + 1).astype(np.float32)
    use_y = jnp.asarray((kind >= 2)[None, :])
    shift = jnp.asarray(np.where(kind % 2 == 1, math.pi / 2, 0.0).astype(np.float32)[None, :])
    position = jnp.where(use_y, offsets[1][:, None], offsets[0][:, None])
    cycles = position * jnp.asarray(freq[None, :])
    cycles = cycles - jnp.round(cycles)
    return jnp.sin(2.0 * math.pi * cycles + shift).astype(BF)


def ring(size, shift):
    return [(i, (i + shift) % size) for i in range(size)]


def halo_rows(latents, noise):
    axes = ("gx", "pa")
    size = lax.axis_size(axes)
    n0, n1 = noise[0], noise[1]
    base = jnp.concatenate([n1[:1], latents, n0, n1[ROWS - 1 :]], axis=0)
    return (
        lax.ppermute(latents[1:], axes, ring(size, 2)),
        lax.ppermute(base[1:], axes, ring(size, 1)),
        latents,
        noise,
        lax.ppermute(base[:-1], axes, ring(size, -1)),
        lax.ppermute(latents[:RAD], axes, ring(size, -2)),
    )


def pack_weights(w_qkv, w_out, w_query, w_head, core):
    pack = jnp.concatenate(
        [
            w_qkv[:, WIDTH:],
            w_qkv[:, :WIDTH],
            w_out,
            w_query.reshape(6, 128),
            jnp.pad(w_head, ((0, 0), (0, 128 - CH))),
        ],
        axis=1,
    )
    mine = lax.dynamic_slice_in_dim(pack, core * HALF, HALF, 1)
    return jnp.broadcast_to(mine[None], (lax.axis_size("gx"),) + mine.shape)


def gather_long(shares):
    return lax.all_to_all(shares, "gx", 0, 0).reshape(192, HALF)


def gather_short(block):
    count = lax.axis_size("pa")
    wide = lax.all_to_all(jnp.broadcast_to(block[None], (count,) + block.shape), "pa", 0, 0)
    return wide.reshape(WIDTH, block.shape[1])


def local(
    latents, noise, proc_gain, w_qkv, w_out, w_query, w_head, probe_cell, probe_offset, probe_count
):
    barrier = lax.optimization_barrier
    cols = lax.axis_size("gy")
    perm_table, pick_table = permutation_tables()
    perm, pick = jnp.asarray(perm_table, BF), jnp.asarray(pick_table, BF)
    gain = proc_gain[None, :]
    core = lax.rem(lax.axis_index("gy"), 2)
    place = jnp.stack([core, probe_count[0]]).astype(jnp.int32)

    shares = pack_weights(w_qkv, w_out, w_query, w_head, core)
    shares, latents, noise = barrier((shares, latents, noise))
    rows = halo_rows(latents, noise)
    block, rows = barrier((gather_long(shares), rows))
    wide = gather_short(block)
    to_high, to_low = run_pack(rows)
    left = lax.ppermute(to_high, "gy", ring(cols, 1))
    right = lax.ppermute(to_low, "gy", ring(cols, -1))
    nk, nq, base, fresh = run_prep(rows, left, right, gain, perm)
    arrays = (nk, nq, base, fresh, features_of(probe_offset), probe_cell[:, None], perm, pick)
    wide, arrays = barrier((wide, arrays))
    other = lax.ppermute(wide, "gy", SWAP)
    latent, probes = run_main(place, gain, arrays, wide, other)
    return latent.reshape(latents.shape), probes


def solution(mesh):
    return jax.shard_map(
        local,
        mesh=mesh,
        in_specs=(
            P(("gx", "pa"), "gy", None),
            P(None, ("gx", "pa"), "gy", None),
            P(),
            P(("gx", "pa"), None),
            P(("gx", "pa"), None),
            P(("gx", "pa"), None),
            P(("gx", "pa"), None),
            P(("gx", "gy", "pa")),
            P(None, ("gx", "gy", "pa")),
            P(("gx", "gy", "pa")),
        ),
        out_specs=(P(("gx", "pa"), "gy", None), P(None, ("gx", "gy", "pa"))),
        check_vma=False,
    )
```

```python
import math

import jax
import jax.numpy as jnp
import numpy as np
from jax import lax
from jax.experimental import pallas as pl
from jax.experimental.pallas import tpu as pltpu
from jax.sharding import PartitionSpec as P

HEADS = 12
FQ = 128
CH = 3
RAD = 3
STEPS = 2
EPS = 1e-06
NOISE_COEF = 0.3

WIDTH = 768
ROWS = 4
COLS = 32
HALO0 = 2 * RAD + 1
HALO1 = RAD + 1
KEY_ROWS = ROWS + 2 * HALO0
EDGE = 8
PITCH0 = COLS + 2 * EDGE
N_EDGE = EDGE * (KEY_ROWS + ROWS + 2 * HALO1 + ROWS + 2)
MID_ROWS = ROWS + 2 * HALO1
PITCH1 = COLS + 2 * HALO1
END_ROWS = ROWS + 2
N_KEY0 = KEY_ROWS * PITCH0
N_MID = MID_ROWS * PITCH1
N_END = END_ROWS * PITCH1
PAIR = 2 * PITCH1
KEYS = 384
HALF = 1664
TAIL = 3 * WIDTH
PARTS = ((0, 0, 768), (0, 768, 768), (0, 1536, 128), (1, 0, 640), (1, 640, 1024))
BLOCK = 128
SWAP = [(0, 1), (1, 0), (2, 3), (3, 2)]
NEG = -1e30
SCALE = math.log2(math.e) / 8.0

BF = jnp.bfloat16
F32 = jnp.float32


def permutation_tables():
    target = np.arange(WIDTH)
    lane, rest = target // 192, target % 192
    source = (rest // 6) * 24 + lane * 6 + rest % 6
    perm = np.zeros((WIDTH, WIDTH), np.float32)
    perm[source, target] = 1.0
    pick = np.zeros((WIDTH, WIDTH), np.float32)
    out = np.arange(WIDTH)
    pick[out, (out % 128) * 6 + out // 128] = 1.0
    return perm, pick


def rms(values, gain):
    factor = lax.rsqrt(jnp.mean(values * values, axis=-1, keepdims=True) + EPS)
    return (values * factor * gain).astype(BF)


def row_lists(far_low, low, own, noise, high, far_high):
    lat = [far_low[r] for r in range(RAD)] + [low[r] for r in range(ROWS)]
    lat += [own[r] for r in range(ROWS)] + [high[1 + r] for r in range(ROWS)]
    lat += [far_high[r] for r in range(RAD)]
    first = [low[ROWS + r] for r in range(ROWS)] + [noise[0, r] for r in range(ROWS)]
    first += [high[1 + ROWS + r] for r in range(ROWS)]
    second = [low[2 * ROWS]] + [noise[1, r] for r in range(ROWS)] + [high[0]]
    return lat, first, second


def pack_kernel(far_low, low, own, noise, high, far_high, to_high, to_low, high_wide, low_wide):
    lists = row_lists(far_low, low, own, noise, high, far_high)
    for i, row in enumerate(lists[0] + lists[1] + lists[2]):
        wide = row.astype(F32)
        high_wide[EDGE * i : EDGE * i + EDGE] = wide[COLS - EDGE :]
        low_wide[EDGE * i : EDGE * i + EDGE] = wide[:EDGE]
    to_high[...] = high_wide[...].astype(BF)
    to_low[...] = low_wide[...].astype(BF)


def prep_kernel(
    far_low,
    low,
    own,
    noise,
    high,
    far_high,
    left_ref,
    right_ref,
    gain_ref,
    perm_ref,
    nk_ref,
    nq_ref,
    base_ref,
    tail_ref,
    left,
    right,
    normed_keys,
    normed_queries,
):
    gain = gain_ref[...]
    lists = row_lists(far_low, low, own, noise, high, far_high)
    left[...] = left_ref[...].astype(F32)
    right[...] = right_ref[...].astype(F32)
    cut = slice(EDGE - HALO1, EDGE + COLS + HALO1)

    def full(i, row):
        span = slice(EDGE * i, EDGE * i + EDGE)
        return jnp.concatenate([left[span], row.astype(F32), right[span]], axis=0)

    for r in range(KEY_ROWS):
        values = full(r, lists[0][r])
        normed = rms(values, gain)
        normed_keys[PITCH0 * r : PITCH0 * r + PITCH0] = normed
        m = r - RAD
        if 0 <= m < MID_ROWS:
            at = slice(PITCH1 * m, PITCH1 * m + PITCH1)
            normed_queries[at] = normed.astype(F32)[cut]
            fresh = full(KEY_ROWS + m, lists[1][m])
            base_ref[at] = (values + NOISE_COEF * fresh)[cut]
    for m in range(END_ROWS):
        fresh = full(KEY_ROWS + MID_ROWS + m, lists[2][m])
        tail_ref[PITCH1 * m : PITCH1 * m + PITCH1] = (NOISE_COEF * fresh)[cut]
    perm = perm_ref[...]
    nk_ref[...] = jnp.dot(normed_keys[...], perm, preferred_element_type=F32).astype(BF)
    nq_ref[...] = jnp.dot(
        normed_queries[...].astype(BF), perm, preferred_element_type=F32
    ).astype(BF)


def stair(index, step, count):
    total = jnp.zeros(index.shape, jnp.int32)
    for i in range(1, count):
        total = total + (index >= step * i).astype(jnp.int32)
    return total


def window_mask(pitch, rows_of_keys):
    row = lax.broadcasted_iota(jnp.int32, (PAIR, KEYS), 0)
    lane = lax.broadcasted_iota(jnp.int32, (PAIR, KEYS), 1)
    q_row = stair(row, PITCH1, 2)
    q_col = row - PITCH1 * q_row
    k_row = stair(lane, pitch, rows_of_keys)
    k_col = lane - pitch * k_row
    return q_row, q_col, k_row, k_col


def attend(queries, keys, values, mask):
    rows = queries.shape[0]
    lane_head = stair(lax.broadcasted_iota(jnp.int32, (rows, 256), 1), 64, 4)
    zero = jnp.zeros((), BF)
    stacked = jnp.concatenate(
        [jnp.where(lane_head == h, queries, zero) for h in range(4)], axis=0
    )
    scores = lax.dot_general(
        stacked, keys, (((1,), (1,)), ((), ())), preferred_element_type=F32
    )
    parts = []
    for h in range(4):
        part = scores[h * rows : (h + 1) * rows] + mask
        top = jnp.max(part, axis=1, keepdims=True)
        weight = jnp.exp2(part - top)
        total = jnp.sum(weight, axis=1, keepdims=True)
        parts.append((weight.astype(BF), 1.0 / total))
    mixed = jnp.dot(
        jnp.concatenate([p[0] for p in parts], axis=0), values, preferred_element_type=F32
    )
    result = mixed[0:rows] * parts[0][1]
    for h in range(1, 4):
        result = jnp.where(
            lane_head == h, mixed[h * rows : (h + 1) * rows] * parts[h][1], result
        )
    return result.astype(BF)


def project(source, weights, column, target, rows, scale=None):
    for t in range(0, WIDTH, 256):
        product = jnp.dot(
            source[...],
            weights[:, column + t : column + t + 256],
            preferred_element_type=F32,
        )
        if scale is not None:
            product = product * scale
        target[0:rows, t : t + 256] = product.astype(BF).astype(target.dtype)


def main_kernel(
    place_ref,
    gain_ref,
    nk_any,
    nq_any,
    base_any,
    noise_any,
    feat_any,
    cell_any,
    perm_any,
    pick_any,
    mine,
    other,
    latent_ref,
    probe_ref,
    weights,
    nk_ref,
    nq_ref,
    base_ref,
    noise_ref,
    feat_ref,
    cell_ref,
    perm_ref,
    pick_ref,
    keys,
    values,
    q_low,
    queries,
    att,
    att_perm,
    lat_mid,
    mid_perm,
    lat_end,
    end_low,
    probe_query,
    part_sems,
    sems,
):
    core = place_ref[0]
    live = place_ref[1]

    def part(ref, n):
        slot, start, width = PARTS[n]
        first = slot * HALF + start
        return pltpu.make_async_copy(
            ref.at[:, start : start + width],
            weights.at[:, first : first + width],
            part_sems.at[n],
        )

    def start_parts(low, high):
        for n, (slot, _, _) in enumerate(PARTS):
            part((low, high)[slot], n).start()

    pairs = (
        (nk_any, nk_ref),
        (nq_any, nq_ref),
        (perm_any, perm_ref),
        (base_any, base_ref),
        (noise_any, noise_ref),
        (pick_any, pick_ref),
        (feat_any, feat_ref),
        (cell_any, cell_ref),
    )
    loads = [pltpu.make_async_copy(a, b, sems.at[n]) for n, (a, b) in enumerate(pairs)]
    loads[0].start()
    pl.when(core == 0)(lambda: start_parts(mine, other))
    pl.when(core != 0)(lambda: start_parts(other, mine))
    for load in loads[1:]:
        load.start()

    q_row, q_col, k_row, k_col = window_mask(PITCH0, 8)
    inside = (
        (k_row >= q_row)
        & (k_row <= q_row + 2 * RAD)
        & (k_col >= q_col + EDGE - HALO1 - RAD)
        & (k_col <= q_col + EDGE - HALO1 + RAD)
    )
    mask = jnp.where(inside, 0.0, NEG).astype(F32)
    loads[0].wait()
    part(mine, 0).wait()
    project(nk_ref, weights, 0, keys, N_KEY0)
    part(mine, 1).wait()
    project(nk_ref, weights, WIDTH, values, N_KEY0)
    loads[1].wait()
    part(mine, 2).wait()
    part(mine, 3).wait()
    project(nq_ref, weights, 2 * WIDTH, q_low, N_MID, SCALE)

    def attend0(j, carry):
        q_at = pl.multiple_of(j * PAIR, PAIR)
        k_at = pl.multiple_of(j * 2 * PITCH0, 2 * PITCH0)
        for g in range(3):
            cols = slice(256 * g, 256 * g + 256)
            att[pl.ds(q_at, PAIR), cols] = attend(
                q_low[pl.ds(q_at, PAIR), cols],
                keys[pl.ds(k_at, KEYS), cols],
                values[pl.ds(k_at, KEYS), cols],
                mask,
            )
        return carry

    lax.fori_loop(0, MID_ROWS // 2, attend0, 0)
    for load in loads[2:]:
        load.wait()
    part(mine, 4).wait()
    att_perm[...] = jnp.dot(att[...], perm_ref[...], preferred_element_type=F32).astype(BF)
    for t in range(3):
        cols = slice(256 * t, 256 * t + 256)
        update = jnp.dot(
            att_perm[...],
            weights[:, TAIL + 256 * t : TAIL + 256 * t + 256],
            preferred_element_type=F32,
        )
        fresh = base_ref[:, cols] + update / STEPS
        lat_mid[:, cols] = fresh.astype(BF).astype(F32)

    mid_perm[...] = jnp.dot(
        rms(lat_mid[...], gain_ref[...]), perm_ref[...], preferred_element_type=F32
    ).astype(BF)
    project(mid_perm, weights, 0, keys, N_MID)
    project(mid_perm, weights, WIDTH, values, N_MID)
    project(mid_perm.at[112:368], weights, 2 * WIDTH, queries, 256, SCALE)

    q_row, q_col, k_row, k_col = window_mask(PITCH1, 10)
    inside = (
        (k_row >= q_row)
        & (k_row <= q_row + 2 * RAD)
        & (k_col >= q_col - RAD)
        & (k_col <= q_col + RAD)
    )
    mask = jnp.where(inside, 0.0, NEG).astype(F32)

    def attend1(j, carry):
        at = pl.multiple_of(j * PAIR, PAIR)
        for g in range(3):
            cols = slice(256 * g, 256 * g + 256)
            att[pl.ds(at, PAIR), cols] = attend(
                queries[pl.ds(pl.multiple_of(at + 8, 8), PAIR), cols].astype(BF),
                keys[pl.ds(at, KEYS), cols],
                values[pl.ds(at, KEYS), cols],
                mask,
            )
        return carry

    lax.fori_loop(0, END_ROWS // 2, attend1, 0)
    att_perm[0:N_END] = jnp.dot(
        att[0:N_END], perm_ref[...], preferred_element_type=F32
    ).astype(BF)

    lat_end[N_END:] = jnp.zeros((256 - N_END, WIDTH), F32)
    for t in range(3):
        cols = slice(256 * t, 256 * t + 256)
        update = jnp.dot(
            att_perm[0:N_END],
            weights[:, TAIL + 256 * t : TAIL + 256 * t + 256],
            preferred_element_type=F32,
        )
        fresh = (
            lat_mid[RAD * PITCH1 : RAD * PITCH1 + N_END, cols]
            + update / STEPS
            + noise_ref[:, cols]
        )
        lat_end[0:N_END, cols] = fresh.astype(BF).astype(F32)
    for r in range(ROWS):
        start = PITCH1 * (r + 1) + HALO1
        latent_ref[COLS * r : COLS * r + COLS] = lat_end[start : start + COLS].astype(BF)

    end_low[...] = lat_end[...].astype(BF)
    query_rows = jnp.dot(
        pick_ref[...], weights[:, TAIL + 768 : TAIL + 896], preferred_element_type=F32
    ).astype(BF)
    for i in range(6):
        probe_query[:, 128 * i : 128 * i + 128] = (
            jnp.dot(
                feat_ref[...], query_rows[128 * i : 128 * i + 128], preferred_element_type=F32
            )
            * SCALE
        ).astype(BF)
    head_rows = jnp.dot(perm_ref[...], weights[:, TAIL + 896 : TAIL + 1024], preferred_element_type=F32)
    head_turned = head_rows.T[0:8].astype(BF)

    spot = lax.broadcasted_iota(jnp.int32, (BLOCK, 256), 1)
    spot_row = stair(spot, PITCH1, 7)
    spot_col = spot - PITCH1 * spot_row

    def decode(b, carry):
        at = pl.multiple_of(b * BLOCK, BLOCK)
        cell = cell_ref[pl.ds(at, BLOCK)]
        cell_row = lax.shift_right_logical(cell, 5)
        cell_col = lax.bitwise_and(cell, 31) + HALO1 - 1
        near = (
            (spot_row >= cell_row)
            & (spot_row <= cell_row + 2)
            & (spot_col >= cell_col)
            & (spot_col <= cell_col + 2)
        )
        near_mask = jnp.where(near, 0.0, NEG).astype(F32)
        mixed = []
        for g in range(3):
            cols = slice(256 * g, 256 * g + 256)
            mixed.append(
                attend(
                    probe_query[pl.ds(at, BLOCK), cols], end_low[:, cols], end_low[:, cols], near_mask
                )
            )
        decoded = lax.dot_general(
            head_turned,
            jnp.concatenate(mixed, axis=1),
            (((1,), (1,)), ((), ())),
            preferred_element_type=F32,
        )
        slot = lax.broadcasted_iota(jnp.int32, (8, BLOCK), 1) + at
        probe_ref[:, pl.ds(at, BLOCK)] = jnp.where(slot < live, decoded, 0.0)[0:CH]
        return carry

    probe_ref[...] = jnp.zeros(probe_ref.shape, F32)
    blocks = lax.div(jnp.clip(live, 0, feat_ref.shape[0]) + BLOCK - 1, BLOCK)
    lax.fori_loop(0, blocks, decode, 0)


def run_pack(rows):
    vmem = pl.BlockSpec(memory_space=pltpu.VMEM)
    return pl.pallas_call(
        pack_kernel,
        out_shape=(jax.ShapeDtypeStruct((N_EDGE, WIDTH), BF),) * 2,
        in_specs=[vmem] * 6,
        out_specs=(vmem,) * 2,
        scratch_shapes=[pltpu.VMEM((N_EDGE, WIDTH), F32)] * 2,
        compiler_params=pltpu.CompilerParams(vmem_limit_bytes=60 * 1024 * 1024),
        cost_estimate=pl.CostEstimate(flops=0, bytes_accessed=3_000_000, transcendentals=0),
        name="pack",
    )(*rows)


def run_prep(rows, left, right, gain, perm):
    vmem = pl.BlockSpec(memory_space=pltpu.VMEM)
    return pl.pallas_call(
        prep_kernel,
        out_shape=(
            jax.ShapeDtypeStruct((N_KEY0, WIDTH), BF),
            jax.ShapeDtypeStruct((N_MID, WIDTH), BF),
            jax.ShapeDtypeStruct((N_MID, WIDTH), F32),
            jax.ShapeDtypeStruct((N_END, WIDTH), F32),
        ),
        in_specs=[vmem] * 10,
        out_specs=(vmem,) * 4,
        scratch_shapes=[
            pltpu.VMEM((N_EDGE, WIDTH), F32),
            pltpu.VMEM((N_EDGE, WIDTH), F32),
            pltpu.VMEM((N_KEY0, WIDTH), BF),
            pltpu.VMEM((N_MID, WIDTH), F32),
        ],
        compiler_params=pltpu.CompilerParams(vmem_limit_bytes=60 * 1024 * 1024),
        cost_estimate=pl.CostEstimate(
            flops=2 * (N_KEY0 + N_MID) * WIDTH * WIDTH, bytes_accessed=8_000_000, transcendentals=0
        ),
        name="prep",
    )(*rows, left, right, gain, perm)


def run_main(place, gain, arrays, mine, other):
    vmem = pl.BlockSpec(memory_space=pltpu.VMEM)
    probes = arrays[5].shape[0]
    return pl.pallas_call(
        main_kernel,
        out_shape=(
            jax.ShapeDtypeStruct((ROWS * COLS, WIDTH), BF),
            jax.ShapeDtypeStruct((CH, probes), F32),
        ),
        in_specs=[pl.BlockSpec(memory_space=pltpu.SMEM), vmem]
        + [pl.BlockSpec(memory_space=pl.ANY)] * (len(arrays) + 2),
        out_specs=(vmem, vmem),
        scratch_shapes=[pltpu.VMEM((WIDTH, 2 * HALF), BF)]
        + [pltpu.VMEM(a.shape, a.dtype) for a in arrays]
        + [
            pltpu.VMEM((N_KEY0, WIDTH), BF),
            pltpu.VMEM((N_KEY0, WIDTH), BF),
            pltpu.VMEM((N_MID, WIDTH), BF),
            pltpu.VMEM((256, WIDTH), F32),
            pltpu.VMEM((N_MID, WIDTH), BF),
            pltpu.VMEM((N_MID, WIDTH), BF),
            pltpu.VMEM((N_MID, WIDTH), F32),
            pltpu.VMEM((N_MID, WIDTH), BF),
            pltpu.VMEM((256, WIDTH), F32),
            pltpu.VMEM((256, WIDTH), BF),
            pltpu.VMEM((probes, WIDTH), BF),
            pltpu.SemaphoreType.DMA((len(PARTS),)),
            pltpu.SemaphoreType.DMA((len(arrays),)),
        ],
        compiler_params=pltpu.CompilerParams(vmem_limit_bytes=60 * 1024 * 1024),
        cost_estimate=pl.CostEstimate(
            flops=16_000_000_000, bytes_accessed=16_000_000, transcendentals=7_000_000
        ),
        name="denoise_decode",
    )(place, gain, *arrays, mine, other)


def features_of(offsets):
    row = np.arange(FQ)
    index = (row % 32) * 4 + row // 32
    kind = index // (FQ // 4)
    freq = (index % (FQ // 4) + 1).astype(np.float32)
    use_y = jnp.asarray((kind >= 2)[None, :])
    shift = jnp.asarray(np.where(kind % 2 == 1, math.pi / 2, 0.0).astype(np.float32)[None, :])
    position = jnp.where(use_y, offsets[1][:, None], offsets[0][:, None])
    cycles = position * jnp.asarray(freq[None, :])
    cycles = cycles - jnp.round(cycles)
    return jnp.sin(2.0 * math.pi * cycles + shift).astype(BF)


def ring(size, shift):
    return [(i, (i + shift) % size) for i in range(size)]


def halo_rows(latents, noise):
    axes = ("gx", "pa")
    size = lax.axis_size(axes)
    n0, n1 = noise[0], noise[1]
    base = jnp.concatenate([n1[:1], latents, n0, n1[ROWS - 1 :]], axis=0)
    return (
        lax.ppermute(latents[1:], axes, ring(size, 2)),
        lax.ppermute(base[1:], axes, ring(size, 1)),
        latents,
        noise,
        lax.ppermute(base[:-1], axes, ring(size, -1)),
        lax.ppermute(latents[:RAD], axes, ring(size, -2)),
    )


def pack_weights(w_qkv, w_out, w_query, w_head, core):
    pack = jnp.concatenate(
        [
            w_qkv[:, WIDTH:],
            w_qkv[:, :WIDTH],
            w_out,
            w_query.reshape(6, 128),
            jnp.pad(w_head, ((0, 0), (0, 128 - CH))),
        ],
        axis=1,
    )
    mine = lax.dynamic_slice_in_dim(pack, core * HALF, HALF, 1)
    return jnp.broadcast_to(mine[None], (lax.axis_size("gx"),) + mine.shape)


def gather_long(shares):
    return lax.all_to_all(shares, "gx", 0, 0).reshape(192, HALF)


def gather_short(block):
    count = lax.axis_size("pa")
    wide = lax.all_to_all(jnp.broadcast_to(block[None], (count,) + block.shape), "pa", 0, 0)
    return wide.reshape(WIDTH, block.shape[1])


def local(
    latents, noise, proc_gain, w_qkv, w_out, w_query, w_head, probe_cell, probe_offset, probe_count
):
    barrier = lax.optimization_barrier
    cols = lax.axis_size("gy")
    perm_table, pick_table = permutation_tables()
    perm, pick = jnp.asarray(perm_table, BF), jnp.asarray(pick_table, BF)
    gain = proc_gain[None, :]
    core = lax.rem(lax.axis_index("gy"), 2)
    place = jnp.stack([core, probe_count[0]]).astype(jnp.int32)

    shares = pack_weights(w_qkv, w_out, w_query, w_head, core)
    shares, latents, noise = barrier((shares, latents, noise))
    rows = halo_rows(latents, noise)
    block, rows = barrier((gather_long(shares), rows))
    wide = gather_short(block)
    to_high, to_low = run_pack(rows)
    left = lax.ppermute(to_high, "gy", ring(cols, 1))
    right = lax.ppermute(to_low, "gy", ring(cols, -1))
    nk, nq, base, fresh = run_prep(rows, left, right, gain, perm)
    arrays = (nk, nq, base, fresh, features_of(probe_offset), probe_cell[:, None], perm, pick)
    wide, arrays = barrier((wide, arrays))
    other = lax.ppermute(wide, "gy", SWAP)
    latent, probes = run_main(place, gain, arrays, wide, other)
    return latent.reshape(latents.shape), probes


def solution(mesh):
    return jax.shard_map(
        local,
        mesh=mesh,
        in_specs=(
            P(("gx", "pa"), "gy", None),
            P(None, ("gx", "pa"), "gy", None),
            P(),
            P(("gx", "pa"), None),
            P(("gx", "pa"), None),
            P(("gx", "pa"), None),
            P(("gx", "pa"), None),
            P(("gx", "gy", "pa")),
            P(None, ("gx", "gy", "pa")),
            P(("gx", "gy", "pa")),
        ),
        out_specs=(P(("gx", "pa"), "gy", None), P(None, ("gx", "gy", "pa"))),
        check_vma=False,
    )
```

```python
import math

import jax
import jax.numpy as jnp
import numpy as np
from jax import lax
from jax.experimental import pallas as pl
from jax.experimental.pallas import tpu as pltpu
from jax.sharding import PartitionSpec as P

HEADS = 12
FQ = 128
CH = 3
RAD = 3
STEPS = 2
EPS = 1e-06
NOISE_COEF = 0.3

WIDTH = 768
ROWS = 4
COLS = 32
HALO0 = 2 * RAD + 1
HALO1 = RAD + 1
KEY_ROWS = ROWS + 2 * HALO0
EDGE = 8
PITCH0 = COLS + 2 * EDGE
N_EDGE = EDGE * (KEY_ROWS + ROWS + 2 * HALO1 + ROWS + 2)
MID_ROWS = ROWS + 2 * HALO1
PITCH1 = COLS + 2 * HALO1
END_ROWS = ROWS + 2
N_KEY0 = KEY_ROWS * PITCH0
N_MID = MID_ROWS * PITCH1
N_END = END_ROWS * PITCH1
PAIR = 2 * PITCH1
KEYS = 384
HALF = 1664
TAIL = 3 * WIDTH
PARTS = ((0, 0, 768), (0, 768, 768), (0, 1536, 128), (1, 0, 640), (1, 640, 1024))
BLOCK = 256
SWAP = [(0, 1), (1, 0), (2, 3), (3, 2)]
NEG = -1e30
SCALE = math.log2(math.e) / 8.0

BF = jnp.bfloat16
F32 = jnp.float32


def permutation_tables():
    target = np.arange(WIDTH)
    lane, rest = target // 192, target % 192
    source = (rest // 6) * 24 + lane * 6 + rest % 6
    perm = np.zeros((WIDTH, WIDTH), np.float32)
    perm[source, target] = 1.0
    pick = np.zeros((WIDTH, WIDTH), np.float32)
    out = np.arange(WIDTH)
    pick[out, (out % 128) * 6 + out // 128] = 1.0
    return perm, pick


def rms(values, gain):
    factor = lax.rsqrt(jnp.mean(values * values, axis=-1, keepdims=True) + EPS)
    return (values * factor * gain).astype(BF)


def row_lists(far_low, low, own, noise, high, far_high):
    lat = [far_low[r] for r in range(RAD)] + [low[r] for r in range(ROWS)]
    lat += [own[r] for r in range(ROWS)] + [high[1 + r] for r in range(ROWS)]
    lat += [far_high[r] for r in range(RAD)]
    first = [low[ROWS + r] for r in range(ROWS)] + [noise[0, r] for r in range(ROWS)]
    first += [high[1 + ROWS + r] for r in range(ROWS)]
    second = [low[2 * ROWS]] + [noise[1, r] for r in range(ROWS)] + [high[0]]
    return lat, first, second


def pack_kernel(far_low, low, own, noise, high, far_high, to_high, to_low, high_wide, low_wide):
    lists = row_lists(far_low, low, own, noise, high, far_high)
    for i, row in enumerate(lists[0] + lists[1] + lists[2]):
        wide = row.astype(F32)
        high_wide[EDGE * i : EDGE * i + EDGE] = wide[COLS - EDGE :]
        low_wide[EDGE * i : EDGE * i + EDGE] = wide[:EDGE]
    to_high[...] = high_wide[...].astype(BF)
    to_low[...] = low_wide[...].astype(BF)


def prep_kernel(
    far_low,
    low,
    own,
    noise,
    high,
    far_high,
    left_ref,
    right_ref,
    gain_ref,
    perm_ref,
    nk_ref,
    nq_ref,
    base_ref,
    tail_ref,
    left,
    right,
    normed_keys,
    normed_queries,
):
    gain = gain_ref[...]
    lists = row_lists(far_low, low, own, noise, high, far_high)
    left[...] = left_ref[...].astype(F32)
    right[...] = right_ref[...].astype(F32)
    cut = slice(EDGE - HALO1, EDGE + COLS + HALO1)

    def full(i, row):
        span = slice(EDGE * i, EDGE * i + EDGE)
        return jnp.concatenate([left[span], row.astype(F32), right[span]], axis=0)

    for r in range(KEY_ROWS):
        values = full(r, lists[0][r])
        normed = rms(values, gain)
        normed_keys[PITCH0 * r : PITCH0 * r + PITCH0] = normed
        m = r - RAD
        if 0 <= m < MID_ROWS:
            at = slice(PITCH1 * m, PITCH1 * m + PITCH1)
            normed_queries[at] = normed.astype(F32)[cut]
            fresh = full(KEY_ROWS + m, lists[1][m])
            base_ref[at] = (values + NOISE_COEF * fresh)[cut]
    for m in range(END_ROWS):
        fresh = full(KEY_ROWS + MID_ROWS + m, lists[2][m])
        tail_ref[PITCH1 * m : PITCH1 * m + PITCH1] = (NOISE_COEF * fresh)[cut]
    perm = perm_ref[...]
    nk_ref[...] = jnp.dot(normed_keys[...], perm, preferred_element_type=F32).astype(BF)
    nq_ref[...] = jnp.dot(
        normed_queries[...].astype(BF), perm, preferred_element_type=F32
    ).astype(BF)


def stair(index, step, count):
    total = jnp.zeros(index.shape, jnp.int32)
    for i in range(1, count):
        total = total + (index >= step * i).astype(jnp.int32)
    return total


def window_mask(pitch, rows_of_keys):
    row = lax.broadcasted_iota(jnp.int32, (PAIR, KEYS), 0)
    lane = lax.broadcasted_iota(jnp.int32, (PAIR, KEYS), 1)
    q_row = stair(row, PITCH1, 2)
    q_col = row - PITCH1 * q_row
    k_row = stair(lane, pitch, rows_of_keys)
    k_col = lane - pitch * k_row
    return q_row, q_col, k_row, k_col


def attend(queries, keys, values, mask):
    rows = queries.shape[0]
    lane_head = stair(lax.broadcasted_iota(jnp.int32, (rows, 256), 1), 64, 4)
    zero = jnp.zeros((), BF)
    stacked = jnp.concatenate(
        [jnp.where(lane_head == h, queries, zero) for h in range(4)], axis=0
    )
    scores = lax.dot_general(
        stacked, keys, (((1,), (1,)), ((), ())), preferred_element_type=F32
    )
    parts = []
    for h in range(4):
        part = scores[h * rows : (h + 1) * rows] + mask
        top = jnp.max(part, axis=1, keepdims=True)
        weight = jnp.exp2(part - top)
        total = jnp.sum(weight, axis=1, keepdims=True)
        parts.append((weight.astype(BF), 1.0 / total))
    mixed = jnp.dot(
        jnp.concatenate([p[0] for p in parts], axis=0), values, preferred_element_type=F32
    )
    result = mixed[0:rows] * parts[0][1]
    for h in range(1, 4):
        result = jnp.where(
            lane_head == h, mixed[h * rows : (h + 1) * rows] * parts[h][1], result
        )
    return result.astype(BF)


def project(source, weights, column, target, rows, scale=None):
    for t in range(0, WIDTH, 256):
        product = jnp.dot(
            source[...],
            weights[:, column + t : column + t + 256],
            preferred_element_type=F32,
        )
        if scale is not None:
            product = product * scale
        target[0:rows, t : t + 256] = product.astype(BF).astype(target.dtype)


def main_kernel(
    place_ref,
    gain_ref,
    nk_any,
    nq_any,
    base_any,
    noise_any,
    feat_any,
    cell_any,
    perm_any,
    pick_any,
    mine,
    other,
    latent_ref,
    probe_ref,
    weights,
    nk_ref,
    nq_ref,
    base_ref,
    noise_ref,
    feat_ref,
    cell_ref,
    perm_ref,
    pick_ref,
    keys,
    values,
    q_low,
    queries,
    att,
    att_perm,
    lat_mid,
    mid_perm,
    lat_end,
    end_low,
    probe_query,
    part_sems,
    sems,
):
    core = place_ref[0]
    live = place_ref[1]

    def part(ref, n):
        slot, start, width = PARTS[n]
        first = slot * HALF + start
        return pltpu.make_async_copy(
            ref.at[:, start : start + width],
            weights.at[:, first : first + width],
            part_sems.at[n],
        )

    def start_parts(low, high):
        for n, (slot, _, _) in enumerate(PARTS):
            part((low, high)[slot], n).start()

    pairs = (
        (nk_any, nk_ref),
        (nq_any, nq_ref),
        (perm_any, perm_ref),
        (base_any, base_ref),
        (noise_any, noise_ref),
        (pick_any, pick_ref),
        (feat_any, feat_ref),
        (cell_any, cell_ref),
    )
    loads = [pltpu.make_async_copy(a, b, sems.at[n]) for n, (a, b) in enumerate(pairs)]
    loads[0].start()
    pl.when(core == 0)(lambda: start_parts(mine, other))
    pl.when(core != 0)(lambda: start_parts(other, mine))
    for load in loads[1:]:
        load.start()

    q_row, q_col, k_row, k_col = window_mask(PITCH0, 8)
    inside = (
        (k_row >= q_row)
        & (k_row <= q_row + 2 * RAD)
        & (k_col >= q_col + EDGE - HALO1 - RAD)
        & (k_col <= q_col + EDGE - HALO1 + RAD)
    )
    mask = jnp.where(inside, 0.0, NEG).astype(F32)
    loads[0].wait()
    part(mine, 0).wait()
    project(nk_ref, weights, 0, keys, N_KEY0)
    part(mine, 1).wait()
    project(nk_ref, weights, WIDTH, values, N_KEY0)
    loads[1].wait()
    part(mine, 2).wait()
    part(mine, 3).wait()
    project(nq_ref, weights, 2 * WIDTH, q_low, N_MID, SCALE)

    def attend0(j, carry):
        q_at = pl.multiple_of(j * PAIR, PAIR)
        k_at = pl.multiple_of(j * 2 * PITCH0, 2 * PITCH0)
        for g in range(3):
            cols = slice(256 * g, 256 * g + 256)
            att[pl.ds(q_at, PAIR), cols] = attend(
                q_low[pl.ds(q_at, PAIR), cols],
                keys[pl.ds(k_at, KEYS), cols],
                values[pl.ds(k_at, KEYS), cols],
                mask,
            )
        return carry

    lax.fori_loop(0, MID_ROWS // 2, attend0, 0, unroll=6)
    for load in loads[2:]:
        load.wait()
    part(mine, 4).wait()
    att_perm[...] = jnp.dot(att[...], perm_ref[...], preferred_element_type=F32).astype(BF)
    for t in range(3):
        cols = slice(256 * t, 256 * t + 256)
        update = jnp.dot(
            att_perm[...],
            weights[:, TAIL + 256 * t : TAIL + 256 * t + 256],
            preferred_element_type=F32,
        )
        fresh = base_ref[:, cols] + update / STEPS
        lat_mid[:, cols] = fresh.astype(BF).astype(F32)

    mid_perm[...] = jnp.dot(
        rms(lat_mid[...], gain_ref[...]), perm_ref[...], preferred_element_type=F32
    ).astype(BF)
    project(mid_perm, weights, 0, keys, N_MID)
    project(mid_perm, weights, WIDTH, values, N_MID)
    project(mid_perm.at[112:368], weights, 2 * WIDTH, queries, 256, SCALE)

    q_row, q_col, k_row, k_col = window_mask(PITCH1, 10)
    inside = (
        (k_row >= q_row)
        & (k_row <= q_row + 2 * RAD)
        & (k_col >= q_col - RAD)
        & (k_col <= q_col + RAD)
    )
    mask = jnp.where(inside, 0.0, NEG).astype(F32)

    def attend1(j, carry):
        at = pl.multiple_of(j * PAIR, PAIR)
        for g in range(3):
            cols = slice(256 * g, 256 * g + 256)
            att[pl.ds(at, PAIR), cols] = attend(
                queries[pl.ds(pl.multiple_of(at + 8, 8), PAIR), cols].astype(BF),
                keys[pl.ds(at, KEYS), cols],
                values[pl.ds(at, KEYS), cols],
                mask,
            )
        return carry

    lax.fori_loop(0, END_ROWS // 2, attend1, 0, unroll=3)
    att_perm[0:N_END] = jnp.dot(
        att[0:N_END], perm_ref[...], preferred_element_type=F32
    ).astype(BF)

    lat_end[N_END:] = jnp.zeros((256 - N_END, WIDTH), F32)
    for t in range(3):
        cols = slice(256 * t, 256 * t + 256)
        update = jnp.dot(
            att_perm[0:N_END],
            weights[:, TAIL + 256 * t : TAIL + 256 * t + 256],
            preferred_element_type=F32,
        )
        fresh = (
            lat_mid[RAD * PITCH1 : RAD * PITCH1 + N_END, cols]
            + update / STEPS
            + noise_ref[:, cols]
        )
        lat_end[0:N_END, cols] = fresh.astype(BF).astype(F32)
    for r in range(ROWS):
        start = PITCH1 * (r + 1) + HALO1
        latent_ref[COLS * r : COLS * r + COLS] = lat_end[start : start + COLS].astype(BF)

    end_low[...] = lat_end[...].astype(BF)
    query_rows = jnp.dot(
        pick_ref[...], weights[:, TAIL + 768 : TAIL + 896], preferred_element_type=F32
    ).astype(BF)
    for i in range(6):
        probe_query[:, 128 * i : 128 * i + 128] = (
            jnp.dot(
                feat_ref[...], query_rows[128 * i : 128 * i + 128], preferred_element_type=F32
            )
            * SCALE
        ).astype(BF)
    head_rows = jnp.dot(perm_ref[...], weights[:, TAIL + 896 : TAIL + 1024], preferred_element_type=F32)
    head_turned = head_rows.T[0:8].astype(BF)

    spot = lax.broadcasted_iota(jnp.int32, (BLOCK, 256), 1)
    spot_row = stair(spot, PITCH1, 7)
    spot_col = spot - PITCH1 * spot_row

    def decode(b, carry):
        at = pl.multiple_of(b * BLOCK, BLOCK)
        cell = cell_ref[pl.ds(at, BLOCK)]
        cell_row = lax.shift_right_logical(cell, 5)
        cell_col = lax.bitwise_and(cell, 31) + HALO1 - 1
        near = (
            (spot_row >= cell_row)
            & (spot_row <= cell_row + 2)
            & (spot_col >= cell_col)
            & (spot_col <= cell_col + 2)
        )
        near_mask = jnp.where(near, 0.0, NEG).astype(F32)
        mixed = []
        for g in range(3):
            cols = slice(256 * g, 256 * g + 256)
            mixed.append(
                attend(
                    probe_query[pl.ds(at, BLOCK), cols], end_low[:, cols], end_low[:, cols], near_mask
                )
            )
        decoded = lax.dot_general(
            head_turned,
            jnp.concatenate(mixed, axis=1),
            (((1,), (1,)), ((), ())),
            preferred_element_type=F32,
        )
        slot = lax.broadcasted_iota(jnp.int32, (8, BLOCK), 1) + at
        probe_ref[:, pl.ds(at, BLOCK)] = jnp.where(slot < live, decoded, 0.0)[0:CH]
        return carry

    probe_ref[...] = jnp.zeros(probe_ref.shape, F32)
    blocks = lax.div(jnp.clip(live, 0, feat_ref.shape[0]) + BLOCK - 1, BLOCK)
    lax.fori_loop(0, blocks, decode, 0)


def run_pack(rows):
    vmem = pl.BlockSpec(memory_space=pltpu.VMEM)
    return pl.pallas_call(
        pack_kernel,
        out_shape=(jax.ShapeDtypeStruct((N_EDGE, WIDTH), BF),) * 2,
        in_specs=[vmem] * 6,
        out_specs=(vmem,) * 2,
        scratch_shapes=[pltpu.VMEM((N_EDGE, WIDTH), F32)] * 2,
        compiler_params=pltpu.CompilerParams(vmem_limit_bytes=60 * 1024 * 1024),
        cost_estimate=pl.CostEstimate(flops=0, bytes_accessed=3_000_000, transcendentals=0),
        name="pack",
    )(*rows)


def run_prep(rows, left, right, gain, perm):
    vmem = pl.BlockSpec(memory_space=pltpu.VMEM)
    return pl.pallas_call(
        prep_kernel,
        out_shape=(
            jax.ShapeDtypeStruct((N_KEY0, WIDTH), BF),
            jax.ShapeDtypeStruct((N_MID, WIDTH), BF),
            jax.ShapeDtypeStruct((N_MID, WIDTH), F32),
            jax.ShapeDtypeStruct((N_END, WIDTH), F32),
        ),
        in_specs=[vmem] * 10,
        out_specs=(vmem,) * 4,
        scratch_shapes=[
            pltpu.VMEM((N_EDGE, WIDTH), F32),
            pltpu.VMEM((N_EDGE, WIDTH), F32),
            pltpu.VMEM((N_KEY0, WIDTH), BF),
            pltpu.VMEM((N_MID, WIDTH), F32),
        ],
        compiler_params=pltpu.CompilerParams(vmem_limit_bytes=60 * 1024 * 1024),
        cost_estimate=pl.CostEstimate(
            flops=2 * (N_KEY0 + N_MID) * WIDTH * WIDTH, bytes_accessed=8_000_000, transcendentals=0
        ),
        name="prep",
    )(*rows, left, right, gain, perm)


def run_main(place, gain, arrays, mine, other):
    vmem = pl.BlockSpec(memory_space=pltpu.VMEM)
    probes = arrays[5].shape[0]
    return pl.pallas_call(
        main_kernel,
        out_shape=(
            jax.ShapeDtypeStruct((ROWS * COLS, WIDTH), BF),
            jax.ShapeDtypeStruct((CH, probes), F32),
        ),
        in_specs=[pl.BlockSpec(memory_space=pltpu.SMEM), vmem]
        + [pl.BlockSpec(memory_space=pl.ANY)] * (len(arrays) + 2),
        out_specs=(vmem, vmem),
        scratch_shapes=[pltpu.VMEM((WIDTH, 2 * HALF), BF)]
        + [pltpu.VMEM(a.shape, a.dtype) for a in arrays]
        + [
            pltpu.VMEM((N_KEY0, WIDTH), BF),
            pltpu.VMEM((N_KEY0, WIDTH), BF),
            pltpu.VMEM((N_MID, WIDTH), BF),
            pltpu.VMEM((256, WIDTH), F32),
            pltpu.VMEM((N_MID, WIDTH), BF),
            pltpu.VMEM((N_MID, WIDTH), BF),
            pltpu.VMEM((N_MID, WIDTH), F32),
            pltpu.VMEM((N_MID, WIDTH), BF),
            pltpu.VMEM((256, WIDTH), F32),
            pltpu.VMEM((256, WIDTH), BF),
            pltpu.VMEM((probes, WIDTH), BF),
            pltpu.SemaphoreType.DMA((len(PARTS),)),
            pltpu.SemaphoreType.DMA((len(arrays),)),
        ],
        compiler_params=pltpu.CompilerParams(vmem_limit_bytes=60 * 1024 * 1024),
        cost_estimate=pl.CostEstimate(
            flops=16_000_000_000, bytes_accessed=16_000_000, transcendentals=7_000_000
        ),
        name="denoise_decode",
    )(place, gain, *arrays, mine, other)


def features_of(offsets):
    row = np.arange(FQ)
    index = (row % 32) * 4 + row // 32
    kind = index // (FQ // 4)
    freq = (index % (FQ // 4) + 1).astype(np.float32)
    use_y = jnp.asarray((kind >= 2)[None, :])
    shift = jnp.asarray(np.where(kind % 2 == 1, math.pi / 2, 0.0).astype(np.float32)[None, :])
    position = jnp.where(use_y, offsets[1][:, None], offsets[0][:, None])
    cycles = position * jnp.asarray(freq[None, :])
    cycles = cycles - jnp.round(cycles)
    return jnp.sin(2.0 * math.pi * cycles + shift).astype(BF)


def ring(size, shift):
    return [(i, (i + shift) % size) for i in range(size)]


def halo_rows(latents, noise):
    axes = ("gx", "pa")
    size = lax.axis_size(axes)
    n0, n1 = noise[0], noise[1]
    base = jnp.concatenate([n1[:1], latents, n0, n1[ROWS - 1 :]], axis=0)
    return (
        lax.ppermute(latents[1:], axes, ring(size, 2)),
        lax.ppermute(base[1:], axes, ring(size, 1)),
        latents,
        noise,
        lax.ppermute(base[:-1], axes, ring(size, -1)),
        lax.ppermute(latents[:RAD], axes, ring(size, -2)),
    )


def pack_weights(w_qkv, w_out, w_query, w_head, core):
    pack = jnp.concatenate(
        [
            w_qkv[:, WIDTH:],
            w_qkv[:, :WIDTH],
            w_out,
            w_query.reshape(6, 128),
            jnp.pad(w_head, ((0, 0), (0, 128 - CH))),
        ],
        axis=1,
    )
    mine = lax.dynamic_slice_in_dim(pack, core * HALF, HALF, 1)
    return jnp.broadcast_to(mine[None], (lax.axis_size("gx"),) + mine.shape)


def gather_long(shares):
    return lax.all_to_all(shares, "gx", 0, 0).reshape(192, HALF)


def gather_short(block):
    count = lax.axis_size("pa")
    wide = lax.all_to_all(jnp.broadcast_to(block[None], (count,) + block.shape), "pa", 0, 0)
    return wide.reshape(WIDTH, block.shape[1])


def local(
    latents, noise, proc_gain, w_qkv, w_out, w_query, w_head, probe_cell, probe_offset, probe_count
):
    barrier = lax.optimization_barrier
    cols = lax.axis_size("gy")
    perm_table, pick_table = permutation_tables()
    perm, pick = jnp.asarray(perm_table, BF), jnp.asarray(pick_table, BF)
    gain = proc_gain[None, :]
    core = lax.rem(lax.axis_index("gy"), 2)
    place = jnp.stack([core, probe_count[0]]).astype(jnp.int32)

    shares = pack_weights(w_qkv, w_out, w_query, w_head, core)
    shares, latents, noise = barrier((shares, latents, noise))
    rows = halo_rows(latents, noise)
    block, rows = barrier((gather_long(shares), rows))
    wide = gather_short(block)
    to_high, to_low = run_pack(rows)
    left = lax.ppermute(to_high, "gy", ring(cols, 1))
    right = lax.ppermute(to_low, "gy", ring(cols, -1))
    nk, nq, base, fresh = run_prep(rows, left, right, gain, perm)
    arrays = (nk, nq, base, fresh, features_of(probe_offset), probe_cell[:, None], perm, pick)
    wide, arrays = barrier((wide, arrays))
    other = lax.ppermute(wide, "gy", SWAP)
    latent, probes = run_main(place, gain, arrays, wide, other)
    return latent.reshape(latents.shape), probes


def solution(mesh):
    return jax.shard_map(
        local,
        mesh=mesh,
        in_specs=(
            P(("gx", "pa"), "gy", None),
            P(None, ("gx", "pa"), "gy", None),
            P(),
            P(("gx", "pa"), None),
            P(("gx", "pa"), None),
            P(("gx", "pa"), None),
            P(("gx", "pa"), None),
            P(("gx", "gy", "pa")),
            P(None, ("gx", "gy", "pa")),
            P(("gx", "gy", "pa")),
        ),
        out_specs=(P(("gx", "pa"), "gy", None), P(None, ("gx", "gy", "pa"))),
        check_vma=False,
    )
```

```python
import math

import jax
import jax.numpy as jnp
import numpy as np
from jax import lax
from jax.experimental import pallas as pl
from jax.experimental.pallas import tpu as pltpu
from jax.sharding import PartitionSpec as P

HEADS = 12
FQ = 128
CH = 3
RAD = 3
STEPS = 2
EPS = 1e-06
NOISE_COEF = 0.3

WIDTH = 768
ROWS = 4
COLS = 32
HALO0 = 2 * RAD + 1
HALO1 = RAD + 1
KEY_ROWS = ROWS + 2 * HALO0
EDGE = 8
PITCH0 = COLS + 2 * EDGE
N_EDGE = EDGE * (KEY_ROWS + ROWS + 2 * HALO1 + ROWS + 2)
MID_ROWS = ROWS + 2 * HALO1
PITCH1 = COLS + 2 * HALO1
END_ROWS = ROWS + 2
N_KEY0 = KEY_ROWS * PITCH0
N_MID = MID_ROWS * PITCH1
N_END = END_ROWS * PITCH1
PAIR = 2 * PITCH1
KEYS = 384
HALF = 1664
TAIL = 3 * WIDTH
PARTS = ((0, 0, 768), (0, 768, 768), (0, 1536, 128), (1, 0, 640), (1, 640, 1024))
BLOCK = 256
SWAP = [(0, 1), (1, 0), (2, 3), (3, 2)]
NEG = -1e30
SCALE = math.log2(math.e) / 8.0

BF = jnp.bfloat16
F32 = jnp.float32


def permutation_tables():
    target = np.arange(WIDTH)
    lane, rest = target // 192, target % 192
    source = (rest // 6) * 24 + lane * 6 + rest % 6
    perm = np.zeros((WIDTH, WIDTH), np.float32)
    perm[source, target] = 1.0
    pick = np.zeros((WIDTH, WIDTH), np.float32)
    out = np.arange(WIDTH)
    pick[out, (out % 128) * 6 + out // 128] = 1.0
    return perm, pick


def rms(values, gain):
    factor = lax.rsqrt(jnp.mean(values * values, axis=-1, keepdims=True) + EPS)
    return (values * factor * gain).astype(BF)


def row_lists(far_low, low, own, noise, high, far_high):
    lat = [far_low[r] for r in range(RAD)] + [low[r] for r in range(ROWS)]
    lat += [own[r] for r in range(ROWS)] + [high[1 + r] for r in range(ROWS)]
    lat += [far_high[r] for r in range(RAD)]
    first = [low[ROWS + r] for r in range(ROWS)] + [noise[0, r] for r in range(ROWS)]
    first += [high[1 + ROWS + r] for r in range(ROWS)]
    second = [low[2 * ROWS]] + [noise[1, r] for r in range(ROWS)] + [high[0]]
    return lat, first, second


def pack_kernel(far_low, low, own, noise, high, far_high, to_high, to_low, high_wide, low_wide):
    lists = row_lists(far_low, low, own, noise, high, far_high)
    for i, row in enumerate(lists[0] + lists[1] + lists[2]):
        wide = row.astype(F32)
        high_wide[EDGE * i : EDGE * i + EDGE] = wide[COLS - EDGE :]
        low_wide[EDGE * i : EDGE * i + EDGE] = wide[:EDGE]
    to_high[...] = high_wide[...].astype(BF)
    to_low[...] = low_wide[...].astype(BF)


def prep_kernel(
    far_low,
    low,
    own,
    noise,
    high,
    far_high,
    left_ref,
    right_ref,
    gain_ref,
    perm_ref,
    nk_ref,
    nq_ref,
    base_ref,
    tail_ref,
    left,
    right,
    normed_keys,
    normed_queries,
):
    gain = gain_ref[...]
    lists = row_lists(far_low, low, own, noise, high, far_high)
    left[...] = left_ref[...].astype(F32)
    right[...] = right_ref[...].astype(F32)
    cut = slice(EDGE - HALO1, EDGE + COLS + HALO1)

    def full(i, row):
        span = slice(EDGE * i, EDGE * i + EDGE)
        return jnp.concatenate([left[span], row.astype(F32), right[span]], axis=0)

    for r in range(KEY_ROWS):
        values = full(r, lists[0][r])
        normed = rms(values, gain)
        normed_keys[PITCH0 * r : PITCH0 * r + PITCH0] = normed
        m = r - RAD
        if 0 <= m < MID_ROWS:
            at = slice(PITCH1 * m, PITCH1 * m + PITCH1)
            normed_queries[at] = normed.astype(F32)[cut]
            fresh = full(KEY_ROWS + m, lists[1][m])
            base_ref[at] = (values + NOISE_COEF * fresh)[cut]
    for m in range(END_ROWS):
        fresh = full(KEY_ROWS + MID_ROWS + m, lists[2][m])
        tail_ref[PITCH1 * m : PITCH1 * m + PITCH1] = (NOISE_COEF * fresh)[cut]
    perm = perm_ref[...]
    nk_ref[...] = jnp.dot(normed_keys[...], perm, preferred_element_type=F32).astype(BF)
    nq_ref[...] = jnp.dot(
        normed_queries[...].astype(BF), perm, preferred_element_type=F32
    ).astype(BF)


def stair(index, step, count):
    total = jnp.zeros(index.shape, jnp.int32)
    for i in range(1, count):
        total = total + (index >= step * i).astype(jnp.int32)
    return total


def window_mask(pitch, rows_of_keys):
    row = lax.broadcasted_iota(jnp.int32, (PAIR, KEYS), 0)
    lane = lax.broadcasted_iota(jnp.int32, (PAIR, KEYS), 1)
    q_row = stair(row, PITCH1, 2)
    q_col = row - PITCH1 * q_row
    k_row = stair(lane, pitch, rows_of_keys)
    k_col = lane - pitch * k_row
    return q_row, q_col, k_row, k_col


def attend(queries, keys, values, mask):
    rows = queries.shape[0]
    lane_head = stair(lax.broadcasted_iota(jnp.int32, (rows, 256), 1), 64, 4)
    zero = jnp.zeros((), BF)
    stacked = jnp.concatenate(
        [jnp.where(lane_head == h, queries, zero) for h in range(4)], axis=0
    )
    scores = lax.dot_general(
        stacked, keys, (((1,), (1,)), ((), ())), preferred_element_type=F32
    )
    parts = []
    for h in range(4):
        part = scores[h * rows : (h + 1) * rows] + mask
        top = jnp.max(part, axis=1, keepdims=True)
        weight = jnp.exp2(part - top)
        total = jnp.sum(weight, axis=1, keepdims=True)
        parts.append((weight.astype(BF), 1.0 / total))
    mixed = jnp.dot(
        jnp.concatenate([p[0] for p in parts], axis=0), values, preferred_element_type=F32
    )
    result = mixed[0:rows] * parts[0][1]
    for h in range(1, 4):
        result = jnp.where(
            lane_head == h, mixed[h * rows : (h + 1) * rows] * parts[h][1], result
        )
    return result.astype(BF)


def project(source, weights, column, target, rows, scale=None):
    for t in range(0, WIDTH, 256):
        product = jnp.dot(
            source[...],
            weights[:, column + t : column + t + 256],
            preferred_element_type=F32,
        )
        if scale is not None:
            product = product * scale
        target[0:rows, t : t + 256] = product.astype(BF).astype(target.dtype)


def main_kernel(
    place_ref,
    gain_ref,
    nk_any,
    nq_any,
    base_any,
    noise_any,
    feat_any,
    cell_any,
    perm_any,
    pick_any,
    mine,
    other,
    latent_ref,
    probe_ref,
    weights,
    nk_ref,
    nq_ref,
    base_ref,
    noise_ref,
    feat_ref,
    cell_ref,
    perm_ref,
    pick_ref,
    keys,
    values,
    q_low,
    queries,
    att,
    att_perm,
    lat_mid,
    mid_perm,
    lat_end,
    end_low,
    probe_query,
    part_sems,
    sems,
):
    core = place_ref[0]
    live = place_ref[1]

    def part(ref, n):
        slot, start, width = PARTS[n]
        first = slot * HALF + start
        return pltpu.make_async_copy(
            ref.at[:, start : start + width],
            weights.at[:, first : first + width],
            part_sems.at[n],
        )

    def start_parts(low, high):
        for n, (slot, _, _) in enumerate(PARTS):
            part((low, high)[slot], n).start()

    pairs = (
        (nk_any, nk_ref),
        (nq_any, nq_ref),
        (perm_any, perm_ref),
        (base_any, base_ref),
        (noise_any, noise_ref),
        (pick_any, pick_ref),
        (feat_any, feat_ref),
        (cell_any, cell_ref),
    )
    loads = [pltpu.make_async_copy(a, b, sems.at[n]) for n, (a, b) in enumerate(pairs)]
    loads[0].start()
    pl.when(core == 0)(lambda: start_parts(mine, other))
    pl.when(core != 0)(lambda: start_parts(other, mine))
    for load in loads[1:]:
        load.start()

    q_row, q_col, k_row, k_col = window_mask(PITCH0, 8)
    inside = (
        (k_row >= q_row)
        & (k_row <= q_row + 2 * RAD)
        & (k_col >= q_col + EDGE - HALO1 - RAD)
        & (k_col <= q_col + EDGE - HALO1 + RAD)
    )
    mask = jnp.where(inside, 0.0, NEG).astype(F32)
    loads[0].wait()
    part(mine, 0).wait()
    project(nk_ref, weights, 0, keys, N_KEY0)
    part(mine, 1).wait()
    project(nk_ref, weights, WIDTH, values, N_KEY0)
    loads[1].wait()
    part(mine, 2).wait()
    part(mine, 3).wait()
    project(nq_ref, weights, 2 * WIDTH, q_low, N_MID, SCALE)

    def attend0(j, carry):
        q_at = pl.multiple_of(j * PAIR, PAIR)
        k_at = pl.multiple_of(j * 2 * PITCH0, 2 * PITCH0)
        for g in range(3):
            cols = slice(256 * g, 256 * g + 256)
            att[pl.ds(q_at, PAIR), cols] = attend(
                q_low[pl.ds(q_at, PAIR), cols],
                keys[pl.ds(k_at, KEYS), cols],
                values[pl.ds(k_at, KEYS), cols],
                mask,
            )
        return carry

    lax.fori_loop(0, MID_ROWS // 2, attend0, 0, unroll=6)
    for load in loads[2:]:
        load.wait()
    part(mine, 4).wait()
    att_perm[...] = jnp.dot(att[...], perm_ref[...], preferred_element_type=F32).astype(BF)
    for t in range(3):
        cols = slice(256 * t, 256 * t + 256)
        update = jnp.dot(
            att_perm[...],
            weights[:, TAIL + 256 * t : TAIL + 256 * t + 256],
            preferred_element_type=F32,
        )
        fresh = base_ref[:, cols] + update / STEPS
        lat_mid[:, cols] = fresh.astype(BF).astype(F32)

    mid_perm[...] = jnp.dot(
        rms(lat_mid[...], gain_ref[...]), perm_ref[...], preferred_element_type=F32
    ).astype(BF)
    project(mid_perm, weights, 0, keys, N_MID)
    project(mid_perm, weights, WIDTH, values, N_MID)
    project(mid_perm.at[112:368], weights, 2 * WIDTH, queries, 256, SCALE)

    q_row, q_col, k_row, k_col = window_mask(PITCH1, 10)
    inside = (
        (k_row >= q_row)
        & (k_row <= q_row + 2 * RAD)
        & (k_col >= q_col - RAD)
        & (k_col <= q_col + RAD)
    )
    mask = jnp.where(inside, 0.0, NEG).astype(F32)

    def attend1(j, carry):
        at = pl.multiple_of(j * PAIR, PAIR)
        for g in range(3):
            cols = slice(256 * g, 256 * g + 256)
            att[pl.ds(at, PAIR), cols] = attend(
                queries[pl.ds(pl.multiple_of(at + 8, 8), PAIR), cols].astype(BF),
                keys[pl.ds(at, KEYS), cols],
                values[pl.ds(at, KEYS), cols],
                mask,
            )
        return carry

    lax.fori_loop(0, END_ROWS // 2, attend1, 0, unroll=3)
    att_perm[0:N_END] = jnp.dot(
        att[0:N_END], perm_ref[...], preferred_element_type=F32
    ).astype(BF)

    lat_end[N_END:] = jnp.zeros((256 - N_END, WIDTH), F32)
    for t in range(3):
        cols = slice(256 * t, 256 * t + 256)
        update = jnp.dot(
            att_perm[0:N_END],
            weights[:, TAIL + 256 * t : TAIL + 256 * t + 256],
            preferred_element_type=F32,
        )
        fresh = (
            lat_mid[RAD * PITCH1 : RAD * PITCH1 + N_END, cols]
            + update / STEPS
            + noise_ref[:, cols]
        )
        lat_end[0:N_END, cols] = fresh.astype(BF).astype(F32)
    for r in range(ROWS):
        start = PITCH1 * (r + 1) + HALO1
        latent_ref[COLS * r : COLS * r + COLS] = lat_end[start : start + COLS].astype(BF)

    end_low[...] = lat_end[...].astype(BF)
    query_rows = jnp.dot(
        pick_ref[...], weights[:, TAIL + 768 : TAIL + 896], preferred_element_type=F32
    ).astype(BF)
    for i in range(6):
        probe_query[:, 128 * i : 128 * i + 128] = (
            jnp.dot(
                feat_ref[...], query_rows[128 * i : 128 * i + 128], preferred_element_type=F32
            )
            * SCALE
        ).astype(BF)
    head_rows = jnp.dot(perm_ref[...], weights[:, TAIL + 896 : TAIL + 1024], preferred_element_type=F32)
    head_turned = head_rows.T[0:8].astype(BF)

    spot = lax.broadcasted_iota(jnp.int32, (BLOCK, 256), 1)
    spot_row = stair(spot, PITCH1, 7)
    spot_col = spot - PITCH1 * spot_row

    def decode(b, carry):
        at = pl.multiple_of(b * BLOCK, BLOCK)
        cell = cell_ref[pl.ds(at, BLOCK)]
        cell_row = lax.shift_right_logical(cell, 5)
        cell_col = lax.bitwise_and(cell, 31) + HALO1 - 1
        near = (
            (spot_row >= cell_row)
            & (spot_row <= cell_row + 2)
            & (spot_col >= cell_col)
            & (spot_col <= cell_col + 2)
        )
        near_mask = jnp.where(near, 0.0, NEG).astype(F32)
        mixed = []
        for g in range(3):
            cols = slice(256 * g, 256 * g + 256)
            mixed.append(
                attend(
                    probe_query[pl.ds(at, BLOCK), cols], end_low[:, cols], end_low[:, cols], near_mask
                )
            )
        decoded = lax.dot_general(
            head_turned,
            jnp.concatenate(mixed, axis=1),
            (((1,), (1,)), ((), ())),
            preferred_element_type=F32,
        )
        slot = lax.broadcasted_iota(jnp.int32, (8, BLOCK), 1) + at
        probe_ref[:, pl.ds(at, BLOCK)] = jnp.where(slot < live, decoded, 0.0)[0:CH]
        return carry

    probe_ref[...] = jnp.zeros(probe_ref.shape, F32)
    blocks = lax.div(jnp.clip(live, 0, feat_ref.shape[0]) + BLOCK - 1, BLOCK)
    lax.fori_loop(0, blocks, decode, 0)


def run_pack(rows):
    vmem = pl.BlockSpec(memory_space=pltpu.VMEM)
    return pl.pallas_call(
        pack_kernel,
        out_shape=(jax.ShapeDtypeStruct((N_EDGE, WIDTH), BF),) * 2,
        in_specs=[vmem] * 6,
        out_specs=(vmem,) * 2,
        scratch_shapes=[pltpu.VMEM((N_EDGE, WIDTH), F32)] * 2,
        compiler_params=pltpu.CompilerParams(vmem_limit_bytes=60 * 1024 * 1024),
        cost_estimate=pl.CostEstimate(flops=0, bytes_accessed=3_000_000, transcendentals=0),
        name="pack",
    )(*rows)


def run_prep(rows, left, right, gain, perm):
    vmem = pl.BlockSpec(memory_space=pltpu.VMEM)
    return pl.pallas_call(
        prep_kernel,
        out_shape=(
            jax.ShapeDtypeStruct((N_KEY0, WIDTH), BF),
            jax.ShapeDtypeStruct((N_MID, WIDTH), BF),
            jax.ShapeDtypeStruct((N_MID, WIDTH), F32),
            jax.ShapeDtypeStruct((N_END, WIDTH), F32),
        ),
        in_specs=[vmem] * 10,
        out_specs=(vmem,) * 4,
        scratch_shapes=[
            pltpu.VMEM((N_EDGE, WIDTH), F32),
            pltpu.VMEM((N_EDGE, WIDTH), F32),
            pltpu.VMEM((N_KEY0, WIDTH), BF),
            pltpu.VMEM((N_MID, WIDTH), F32),
        ],
        compiler_params=pltpu.CompilerParams(vmem_limit_bytes=60 * 1024 * 1024),
        cost_estimate=pl.CostEstimate(
            flops=2 * (N_KEY0 + N_MID) * WIDTH * WIDTH, bytes_accessed=8_000_000, transcendentals=0
        ),
        name="prep",
    )(*rows, left, right, gain, perm)


def run_main(place, gain, arrays, mine, other):
    vmem = pl.BlockSpec(memory_space=pltpu.VMEM)
    probes = arrays[5].shape[0]
    return pl.pallas_call(
        main_kernel,
        out_shape=(
            jax.ShapeDtypeStruct((ROWS * COLS, WIDTH), BF),
            jax.ShapeDtypeStruct((CH, probes), F32),
        ),
        in_specs=[pl.BlockSpec(memory_space=pltpu.SMEM), vmem]
        + [pl.BlockSpec(memory_space=pl.ANY)] * (len(arrays) + 2),
        out_specs=(vmem, vmem),
        scratch_shapes=[pltpu.VMEM((WIDTH, 2 * HALF), BF)]
        + [pltpu.VMEM(a.shape, a.dtype) for a in arrays]
        + [
            pltpu.VMEM((N_KEY0, WIDTH), BF),
            pltpu.VMEM((N_KEY0, WIDTH), BF),
            pltpu.VMEM((N_MID, WIDTH), BF),
            pltpu.VMEM((256, WIDTH), F32),
            pltpu.VMEM((N_MID, WIDTH), BF),
            pltpu.VMEM((N_MID, WIDTH), BF),
            pltpu.VMEM((N_MID, WIDTH), F32),
            pltpu.VMEM((N_MID, WIDTH), BF),
            pltpu.VMEM((256, WIDTH), F32),
            pltpu.VMEM((256, WIDTH), BF),
            pltpu.VMEM((probes, WIDTH), BF),
            pltpu.SemaphoreType.DMA((len(PARTS),)),
            pltpu.SemaphoreType.DMA((len(arrays),)),
        ],
        compiler_params=pltpu.CompilerParams(vmem_limit_bytes=60 * 1024 * 1024),
        cost_estimate=pl.CostEstimate(
            flops=16_000_000_000, bytes_accessed=16_000_000, transcendentals=7_000_000
        ),
        name="denoise_decode",
    )(place, gain, *arrays, mine, other)


def features_of(offsets):
    row = np.arange(FQ)
    index = (row % 32) * 4 + row // 32
    kind = index // (FQ // 4)
    freq = (index % (FQ // 4) + 1).astype(np.float32)
    use_y = jnp.asarray((kind >= 2)[None, :])
    shift = jnp.asarray(np.where(kind % 2 == 1, math.pi / 2, 0.0).astype(np.float32)[None, :])
    position = jnp.where(use_y, offsets[1][:, None], offsets[0][:, None])
    cycles = position * jnp.asarray(freq[None, :])
    cycles = cycles - jnp.round(cycles)
    return jnp.sin(2.0 * math.pi * cycles + shift).astype(BF)


def ring(size, shift):
    return [(i, (i + shift) % size) for i in range(size)]


def halo_rows(latents, noise):
    axes = ("gx", "pa")
    size = lax.axis_size(axes)
    n0, n1 = noise[0], noise[1]
    base = jnp.concatenate([n1[:1], latents, n0, n1[ROWS - 1 :]], axis=0)
    return (
        lax.ppermute(latents[1:], axes, ring(size, 2)),
        lax.ppermute(base[1:], axes, ring(size, 1)),
        latents,
        noise,
        lax.ppermute(base[:-1], axes, ring(size, -1)),
        lax.ppermute(latents[:RAD], axes, ring(size, -2)),
    )


def pack_weights(w_qkv, w_out, w_query, w_head, core):
    pack = jnp.concatenate(
        [
            w_qkv[:, WIDTH:],
            w_qkv[:, :WIDTH],
            w_out,
            w_query.reshape(6, 128),
            jnp.pad(w_head, ((0, 0), (0, 128 - CH))),
        ],
        axis=1,
    )
    mine = lax.dynamic_slice_in_dim(pack, core * HALF, HALF, 1)
    return jnp.broadcast_to(mine[None], (lax.axis_size("gx"),) + mine.shape)


def gather_long(shares):
    return lax.all_to_all(shares, "gx", 0, 0).reshape(192, HALF)


def gather_short(block):
    count = lax.axis_size("pa")
    wide = lax.all_to_all(jnp.broadcast_to(block[None], (count,) + block.shape), "pa", 0, 0)
    return wide.reshape(WIDTH, block.shape[1])


def local(
    latents, noise, proc_gain, w_qkv, w_out, w_query, w_head, probe_cell, probe_offset, probe_count
):
    barrier = lax.optimization_barrier
    cols = lax.axis_size("gy")
    perm_table, pick_table = permutation_tables()
    perm, pick = jnp.asarray(perm_table, BF), jnp.asarray(pick_table, BF)
    gain = proc_gain[None, :]
    core = lax.rem(lax.axis_index("gy"), 2)
    place = jnp.stack([core, probe_count[0]]).astype(jnp.int32)

    shares = pack_weights(w_qkv, w_out, w_query, w_head, core)
    shares, latents, noise = barrier((shares, latents, noise))
    rows = halo_rows(latents, noise)
    rows = list(rows)
    block, rows[1], rows[4] = barrier((gather_long(shares), rows[1], rows[4]))
    wide = gather_short(block)
    to_high, to_low = run_pack(rows)
    left = lax.ppermute(to_high, "gy", ring(cols, 1))
    right = lax.ppermute(to_low, "gy", ring(cols, -1))
    nk, nq, base, fresh = run_prep(rows, left, right, gain, perm)
    arrays = (nk, nq, base, fresh, features_of(probe_offset), probe_cell[:, None], perm, pick)
    wide, arrays = barrier((wide, arrays))
    other = lax.ppermute(wide, "gy", SWAP)
    latent, probes = run_main(place, gain, arrays, wide, other)
    return latent.reshape(latents.shape), probes


def solution(mesh):
    return jax.shard_map(
        local,
        mesh=mesh,
        in_specs=(
            P(("gx", "pa"), "gy", None),
            P(None, ("gx", "pa"), "gy", None),
            P(),
            P(("gx", "pa"), None),
            P(("gx", "pa"), None),
            P(("gx", "pa"), None),
            P(("gx", "pa"), None),
            P(("gx", "gy", "pa")),
            P(None, ("gx", "gy", "pa")),
            P(("gx", "gy", "pa")),
        ),
        out_specs=(P(("gx", "pa"), "gy", None), P(None, ("gx", "gy", "pa"))),
        check_vma=False,
    )
```
